128 devices in a mesh: dp: 8 (over z, core), mp: 16 (over x, y).
Axes of the slice: x: 4, y: 4, z: 4, core: 2. Of those that a mesh axis runs over, the one named last changes fastest.
Arguments:
- hidden_in: bfloat16 [32768, 2048], P(('dp', 'mp')), may hold values from -6 to 6
- mlp_gain: bfloat16 [2048], replicated, may hold values from 0.25 to 1.75
- w_gate: bfloat16 [2048, 5504], P(None, 'mp'), may hold values from -0.125 to 0.125
- w_up: bfloat16 [2048, 5504], P(None, 'mp'), may hold values from -0.125 to 0.125
- w_down: bfloat16 [5504, 2048], P('mp'), may hold values from -0.078125 to 0.078125
- lengths: int32 [1024], P(('dp', 'mp')), may hold values from 1 to 32
- file_cluster: int32 [1024], P(('dp', 'mp')), may hold values from 0 to 127, as said below
- file_order: int32 [1024], P(('dp', 'mp')), may hold values from 0 to 1048575
- cluster_slot: int32 [128], replicated, may hold values from 0 to 127, as said below
- bank: bfloat16 [262144, 2048], P(('dp', 'mp')), may hold values from -0.125 to 0.125
- bank_slot: int32 [262144], P(('dp', 'mp')), may hold values from 0 to 15
- bank_order: int32 [262144], P(('dp', 'mp')), may hold values from 0 to 1048575
- centroid_old: float32 [128, 2048], P(('dp', 'mp')), may hold values from -0.125 to 0.125
- count_old: float32 [128], P(('dp', 'mp')), may hold values from 1 to 8
Outputs:
- max_sim: float32 [1024], P(('dp', 'mp'))
- centroid_new: float32 [128, 2048], P(('dp', 'mp'))
The draws below stay inside these ranges and needn't reach their ends.
Inputs may be any that keep to these rules, and one draw needn't show every extreme that they name: `file_cluster`: the files of one device have at most 2 slots in any one owner's range of 16 slots; the first device has exactly 2 files in one range. `cluster_slot`: A permutation of the 128 slots.
All inputs are finite; a program needn't handle non-finite values.
Results may differ from the reference program's by a relative error of at most 0.0023.
Values may be sent and summed in bfloat16 or wider, within the bound.
No kernel may reach another device: no remote copies, remote signals or barrier semaphores. Data moves between devices by JAX's collectives and lax.ppermute only.
A program may use at most 192 MiB of HBM per device.

```python
import math
import jax
import jax.numpy as jnp
from jax import lax

D = 2048
FF = 5504
FLEN = 32
FILES_DEV = 8
BANK_DEV = 2048
KO = 16
TOK_DEV = 256
TOKENS = 32768
FILES = 1024
BANK = 262144
K = 128
N_DP = 8
N_MP = 16


def cluster_table(key):
    return jax.random.permutation(key, K)


def draw_cluster_slot(key, part):
    table = cluster_table(key)
    return jnp.argsort(table).astype(jnp.int32)


def draw_file_cluster(key, part):
    table = cluster_table(key)
    key = jax.random.fold_in(key, 12)
    key_perm, key_flag, key_local = jax.random.split(key, 3)
    blocks = N_DP * N_MP
    limit = min(2, FILES_DEV)
    owner_pool = jnp.repeat(jnp.arange(N_DP, dtype=jnp.int32), limit)

    def one_block(block_key):
        return jax.random.permutation(block_key, owner_pool)[:FILES_DEV]
    owners = jax.vmap(one_block)(jax.random.split(key_perm, blocks))
    if FILES_DEV > 1:
        flags = jax.random.randint(key_flag, (blocks,), 0, 2)
        flags = flags.at[0].set(1)
        leader = owners[:, 0]
        elsewhere = jnp.sum((owners[:, 2:] == leader[:, None]).astype(jnp.int32), axis=1) > 0
        second = jnp.where((flags == 1) & jnp.logical_not(elsewhere), leader, owners[:, 1])
        owners = owners.at[:, 1].set(second)
    local = jax.random.randint(key_local, (blocks, FILES_DEV), 0, KO)
    clusters = table[owners * KO + local]
    return clusters.reshape(-1).astype(jnp.int32)


def with_ends(drawn, own_key, smallest, top_value):
    longest = drawn.shape.index(max(drawn.shape))
    spots = []
    for shift in (0, 1):
        where = [jax.random.randint(jax.random.fold_in(own_key, axis), (), 0, length) for axis, length in enumerate(drawn.shape)]
        where[longest] = (where[longest] + shift) % drawn.shape[longest]
        spots.append(tuple(where))
    return drawn.at[spots[0]].set(smallest).at[spots[1]].set(top_value)


def steps_of(stream_key, shape, pieces, smallest, top_value):
    loudness, own = 1.0, jax.random.fold_in(stream_key, 6)
    for position, shards_of in pieces:
        steps = jnp.exp(jax.random.uniform(jax.random.fold_in(own, position), (shards_of,), jnp.float32, smallest / len(pieces), top_value / len(pieces)))
        loudness = loudness * jnp.repeat(steps, shape[position] // shards_of).reshape([-1 if axis == position else 1 for axis in range(len(shape))])
    return loudness


def bell_draw(stream_key, extent, spread, reach, pieces=(), kind=jnp.bfloat16):
    loudness = steps_of(stream_key, extent, pieces, -0.22, 0.18) if pieces else 1.0
    values = jax.random.normal(stream_key, extent, jnp.float32) * spread * loudness
    return jnp.minimum(jnp.maximum(values, -reach), reach).astype(kind)


def setup_inputs(seed: int = 0) -> dict:
    streams_of = jax.random.split(jax.random.key(seed), 15)
    return {
        "hidden_in": bell_draw(streams_of[0], (TOKENS, D), 1.0, 6.0, ((0, 128),)),
        "mlp_gain": jnp.clip(1.0 + 0.15 * jax.random.normal(streams_of[1], (D,), jnp.float32), 0.25, 1.75).astype(jnp.bfloat16),
        "w_gate": bell_draw(streams_of[2], (D, FF), D ** -0.5, 0.125, ((1, 16),)),
        "w_up": bell_draw(streams_of[3], (D, FF), D ** -0.5, 0.125, ((1, 16),)),
        "w_down": bell_draw(streams_of[4], (FF, D), FF ** -0.5, 0.078125, ((0, 16),)),
        "lengths": with_ends(jax.random.randint(streams_of[5], (FILES,), 1, FLEN + 1), jax.random.fold_in(streams_of[5], 1), 1, FLEN).astype(jnp.int32),
        "file_cluster": draw_file_cluster(jax.random.fold_in(streams_of[14], 71), 0),
        "file_order": with_ends(jax.random.randint(streams_of[7], (FILES,), 0, 1048576), jax.random.fold_in(streams_of[7], 1), 0, 1048575).astype(jnp.int32),
        "cluster_slot": draw_cluster_slot(jax.random.fold_in(streams_of[14], 71), 0),
        "bank": bell_draw(streams_of[9], (BANK, D), D ** -0.5, 0.125, ((0, 128),)),
        "bank_slot": with_ends(jax.random.randint(streams_of[10], (BANK,), 0, KO), jax.random.fold_in(streams_of[10], 1), 0, KO - 1).astype(jnp.int32),
        "bank_order": with_ends(jax.random.randint(streams_of[11], (BANK,), 0, 1048576), jax.random.fold_in(streams_of[11], 1), 0, 1048575).astype(jnp.int32),
        "centroid_old": bell_draw(streams_of[12], (K, D), D ** -0.5, 0.125, ((0, 128),), jnp.float32),
        "count_old": jnp.clip(jnp.exp(math.log(8.0) - 2.0794415 * jax.random.uniform(streams_of[13], (K,), jnp.float32) ** steps_of(streams_of[13], (K,), ((0, 128),), -0.2, 0.2)), 1.0, 8.0),
    }


def reference(hidden_in, mlp_gain, w_gate, w_up, w_down, lengths, file_cluster, file_order, cluster_slot, bank, bank_slot, bank_order, centroid_old, count_old):
    gain = mlp_gain.astype(jnp.float32)

    def embed_one(args):
        block, lens = args
        resid = block.astype(jnp.float32)
        scale = lax.rsqrt(lax.optimization_barrier(jnp.mean(resid * resid, axis=-1, keepdims=True)) + 1e-05)
        normed = (resid * scale * gain).astype(jnp.bfloat16)
        gate = jnp.dot(normed, w_gate, preferred_element_type=jnp.float32)
        upper = jnp.dot(normed, w_up, preferred_element_type=jnp.float32)
        units = (jax.nn.silu(gate) * upper).astype(jnp.bfloat16)
        mixed = resid + jnp.dot(units, w_down, preferred_element_type=jnp.float32)
        valid = (jnp.arange(FLEN)[None, :] < lens[:, None]).astype(jnp.float32)
        pooled = lax.optimization_barrier(jnp.sum(mixed.reshape(FILES_DEV, FLEN, D) * valid[:, :, None], axis=1))
        pooled = pooled / lens.astype(jnp.float32)[:, None]
        emb = pooled * lax.rsqrt(lax.optimization_barrier(jnp.sum(pooled * pooled, axis=-1, keepdims=True)) + 1e-06)
        return emb.astype(jnp.bfloat16)
    embs = lax.map(embed_one, (hidden_in.reshape(-1, TOK_DEV, D), lengths.reshape(-1, FILES_DEV))).reshape(FILES, D)
    slot = cluster_slot[file_cluster].astype(jnp.int32)
    owner = slot // KO
    local = slot % KO
    group_bank = bank.reshape(N_DP, N_MP * BANK_DEV, D)
    group_slot = bank_slot.reshape(N_DP, N_MP * BANK_DEV)
    group_order = bank_order.reshape(N_DP, N_MP * BANK_DEV)

    def group_best(args):
        rows, slots, orders, index = args
        sims = jnp.dot(embs, rows.T, preferred_element_type=jnp.float32)
        valid = (owner[:, None] == index) & (slots[None, :] == local[:, None]) & (orders[None, :] < file_order[:, None])
        return lax.optimization_barrier(jnp.max(jnp.where(valid, sims, jnp.float32(-1.0)), axis=1))
    best = lax.map(group_best, (group_bank, group_slot, group_order, jnp.arange(N_DP, dtype=jnp.int32)))
    max_sim = lax.optimization_barrier(jnp.max(best, axis=0))
    onehot = (slot[None, :] == jnp.arange(K, dtype=jnp.int32)[:, None]).astype(jnp.float32)
    sums = jnp.dot(onehot, embs.astype(jnp.float32), precision=lax.Precision.HIGHEST)
    counts = lax.optimization_barrier(jnp.sum(onehot, axis=1))
    centroid_new = (count_old[:, None] * centroid_old + sums) / (count_old + counts)[:, None]
    return (max_sim, centroid_new)
```

```python
import functools

import jax
import jax.numpy as jnp
from jax import lax
from jax.experimental import pallas as pl
from jax.experimental.pallas import tpu as pltpu
from jax.sharding import PartitionSpec as P

ALL = ("dp", "mp")
NX, NY, NZ, NC = 4, 4, 4, 2
BF, F32, I32 = jnp.bfloat16, jnp.float32, jnp.int32
VMEM = pltpu.CompilerParams(vmem_limit_bytes=56 * 1024 * 1024)
NT = (((1,), (1,)), ((), ()))


def from_x(v, j):
    perm = [(((x + j) % NX) * NY + y, x * NY + y) for x in range(NX) for y in range(NY)]
    return lax.ppermute(v, "mp", perm)


def from_y(v, k):
    perm = [(x * NY + (y + k) % NY, x * NY + y) for x in range(NX) for y in range(NY)]
    return lax.ppermute(v, "mp", perm)


def from_z(v, k):
    perm = [(((z + k) % NZ) * NC + c, z * NC + c) for z in range(NZ) for c in range(NC)]
    return lax.ppermute(v, "dp", perm)


def from_core(v):
    return lax.ppermute(v, "dp", [(d ^ 1, d) for d in range(NZ * NC)])


def block_ones(files, file_len, dtype):
    row = lax.broadcasted_iota(I32, (files, files * file_len), 0)
    col = lax.broadcasted_iota(I32, (files, files * file_len), 1)
    return jnp.where(col // file_len == row, 1.0, 0.0).astype(dtype)


def prep_kernel(file_len, h_ref, gain_ref, mask_ref, n_ref, p_ref):
    resid = h_ref[...].astype(F32)
    scale = lax.rsqrt(jnp.mean(resid * resid, axis=-1, keepdims=True) + 1e-05)
    normed = resid * scale * gain_ref[...].astype(F32)
    keep = mask_ref[...] > 0.5
    n_ref[...] = jnp.where(keep, normed, 0.0).astype(BF)
    files = p_ref.shape[0]
    valid = jnp.where(keep, resid, 0.0).astype(BF)
    p_ref[...] = jnp.dot(block_ones(files, file_len, BF), valid, preferred_element_type=F32)


def prep(hidden, gain, mask, files):
    tok, width = hidden.shape
    return pl.pallas_call(
        functools.partial(prep_kernel, tok // files),
        out_shape=(jax.ShapeDtypeStruct((tok, width), BF), jax.ShapeDtypeStruct((files, width), F32)),
        compiler_params=VMEM,
        name="prep",
    )(hidden, gain[None, :], mask)


def ffn_kernel(n_tok, n_slices, n_parts, files, off_ref, *refs):
    toks = refs[:n_tok]
    parts = refs[n_tok:n_tok + n_slices * n_parts]
    outs = refs[n_tok + n_slices * n_parts:n_tok + n_slices * n_parts + n_slices]
    t_buf, w_buf, t_sem, w_sem = refs[n_tok + n_slices * n_parts + n_slices:]
    tok = toks[0].shape[0]
    half = w_buf.shape[2] // 2
    w_copies = []
    t_copies = []
    for s in range(n_slices):
        row = []
        for p in range(n_parts):
            src = parts[s * n_parts + p]
            rows = src.shape[0]
            start = pl.multiple_of(off_ref[s * n_parts + p], 256)
            cp = pltpu.make_async_copy(src, w_buf.at[s, pl.ds(start, rows)], w_sem.at[s, p])
            cp.start()
            row.append(cp)
        w_copies.append(row)
        if s == 0:
            for t in range(n_tok):
                cp = pltpu.make_async_copy(toks[t], t_buf.at[pl.ds(t * tok, tok)], t_sem.at[t])
                cp.start()
                t_copies.append(cp)
    ones = block_ones(files, tok // files, BF)
    for s in range(n_slices):
        for cp in w_copies[s]:
            cp.wait()
        for t in range(n_tok):
            if s == 0:
                t_copies[t].wait()
            x = t_buf[t * tok:(t + 1) * tok, :]
            both = jnp.dot(x, w_buf[s], preferred_element_type=F32)
            gate = both[:, :half]
            units = (gate / (1.0 + jnp.exp(-gate)) * both[:, half:]).astype(BF)
            outs[s][t * files:(t + 1) * files, :] = jnp.dot(ones, units, preferred_element_type=F32)


def ffn(toks, slices, offs, files, name):
    n_tok, n_slices, n_parts = len(toks), len(slices), len(slices[0])
    tok, width = toks[0].shape
    cols = slices[0][0].shape[1]
    flat = [p for s in slices for p in s]
    anyspec = pl.BlockSpec(memory_space=pl.ANY)
    out = jax.ShapeDtypeStruct((n_tok * files, cols // 2), F32)
    return pl.pallas_call(
        functools.partial(ffn_kernel, n_tok, n_slices, n_parts, files),
        in_specs=[pl.BlockSpec(memory_space=pltpu.SMEM)] + [anyspec] * (n_tok + len(flat)),
        out_specs=tuple(pl.BlockSpec(memory_space=pltpu.VMEM) for _ in slices),
        out_shape=tuple(out for _ in slices),
        scratch_shapes=[
            pltpu.VMEM((n_tok * tok, width), BF),
            pltpu.VMEM((n_slices, width, cols), BF),
            pltpu.SemaphoreType.DMA((n_tok,)),
            pltpu.SemaphoreType.DMA((n_slices, n_parts)),
        ],
        compiler_params=VMEM,
        name=name,
    )(offs, *toks, *flat)


def down_kernel(files, pos_ref, u0, u1, u2, u3, w_ref, o_ref, buf):
    for k, u in enumerate((u0, u1, u2, u3)):
        for j in range(NX):
            dst = pl.multiple_of(pos_ref[k * NX + j], files)
            buf[pl.ds(dst, files), :] = u[j * files:(j + 1) * files, :]
    hid = w_ref.shape[0]
    rows = buf[:, :hid]
    hi = rows.astype(BF)
    lo = (rows - hi.astype(F32)).astype(BF)
    w = w_ref[...]
    o_ref[...] = jnp.dot(hi, w, preferred_element_type=F32) + jnp.dot(lo, w, preferred_element_type=F32)


def down(us, w_down, pos, files):
    rows = NX * NY * files
    vm = pl.BlockSpec(memory_space=pltpu.VMEM)
    return pl.pallas_call(
        functools.partial(down_kernel, files),
        in_specs=[pl.BlockSpec(memory_space=pltpu.SMEM)] + [vm] * 5,
        out_specs=vm,
        out_shape=jax.ShapeDtypeStruct((rows, w_down.shape[1]), F32),
        scratch_shapes=[pltpu.VMEM((rows, us[0].shape[1]), F32)],
        compiler_params=VMEM,
        name="down",
    )(pos, *us, w_down)


def emb_kernel(files, t_ref, p_ref, len_ref, o_ref):
    total = p_ref[...]
    for m in range(t_ref.shape[0] // files):
        total = total + t_ref[m * files:(m + 1) * files, :]
    pooled = total / len_ref[...]
    norm = lax.rsqrt(jnp.sum(pooled * pooled, axis=-1, keepdims=True) + 1e-06)
    o_ref[...] = (pooled * norm).astype(BF)


def emb_of(terms, pooled, lens, files):
    return pl.pallas_call(
        functools.partial(emb_kernel, files),
        out_shape=jax.ShapeDtypeStruct(pooled.shape, BF),
        compiler_params=VMEM,
        name="emb",
    )(terms, pooled, lens)


def spread_kernel(emb_ref, sel_ref, o_ref):
    o_ref[...] = jnp.dot(sel_ref[...], emb_ref[...], preferred_element_type=F32).astype(BF)


def spread(emb, sel):
    return pl.pallas_call(
        spread_kernel,
        out_shape=jax.ShapeDtypeStruct((sel.shape[0], emb.shape[1]), BF),
        compiler_params=VMEM,
        name="spread",
    )(emb, sel)


def match_kernel(rows_ref, lp_ref, ord_ref, mem_ref, bank_ref, slot_ref, border_ref, best_ref, sums_ref, acc):
    step = pl.program_id(0)

    @pl.when(step == 0)
    def _():
        acc[...] = jnp.full(acc.shape, -1.0, F32)
        sums_ref[...] = jnp.dot(mem_ref[...], rows_ref[...], preferred_element_type=F32)

    sims = lax.dot_general(rows_ref[...], bank_ref[...], NT, preferred_element_type=F32)
    valid = (slot_ref[...] + 1 == lp_ref[...]) & (border_ref[...] < ord_ref[...])
    acc[...] = jnp.maximum(acc[...], jnp.where(valid, sims, -1.0))

    @pl.when(step == pl.num_programs(0) - 1)
    def _():
        best_ref[...] = jnp.max(acc[...], axis=1, keepdims=True)


def match(rows, lp, order, member, bank, bank_slot, bank_order):
    n, width = rows.shape
    block = 512
    whole = lambda shape: pl.BlockSpec(shape, lambda i: (0, 0))
    return pl.pallas_call(
        match_kernel,
        grid=(bank.shape[0] // block,),
        in_specs=[
            whole((n, width)),
            whole((n, 1)),
            whole((n, 1)),
            whole(member.shape),
            pl.BlockSpec((block, width), lambda i: (i, 0)),
            pl.BlockSpec((1, block), lambda i: (0, i)),
            pl.BlockSpec((1, block), lambda i: (0, i)),
        ],
        out_specs=(whole((n, 1)), whole((member.shape[0], width))),
        out_shape=(jax.ShapeDtypeStruct((n, 1), F32), jax.ShapeDtypeStruct((member.shape[0], width), F32)),
        scratch_shapes=[pltpu.VMEM((n, block), F32)],
        compiler_params=VMEM,
        name="match",
    )(rows, lp, order, member, bank, bank_slot[None, :], bank_order[None, :])


def on_device(
    hidden_in,
    mlp_gain,
    w_gate,
    w_up,
    w_down,
    lengths,
    file_cluster,
    file_order,
    cluster_slot,
    bank,
    bank_slot,
    bank_order,
    centroid_old,
    count_old,
):
    tok, width = hidden_in.shape
    files = lengths.shape[0]
    file_len = tok // files
    n_dp, n_mp = NZ * NC, NX * NY
    hid = w_gate.shape[1]
    lanes = -(-hid // 128) * 128
    dp, mp = lax.axis_index("dp"), lax.axis_index("mp")
    z, c, x, y = dp // NC, dp % NC, mp // NY, mp % NY

    def packed(start, rows):
        pad = ((0, 0), (0, lanes - hid))
        g = jnp.pad(lax.dynamic_slice_in_dim(w_gate, start, rows, 0), pad)
        u = jnp.pad(lax.dynamic_slice_in_dim(w_up, start, rows, 0), pad)
        return jnp.concatenate([g, u], axis=1)

    eighth, half = width // 8, width // 2
    w_e = packed(dp * eighth, eighth)
    w_h = packed(c * half, half)
    e0 = from_y(w_e, 2)
    h1, h3 = from_y(w_h, 1), from_y(w_h, 3)

    mask = (jnp.arange(file_len, dtype=I32)[None, :] < lengths[:, None]).astype(F32).reshape(tok, 1)
    normed, pooled_in = prep(hidden_in, mlp_gain, mask, files)
    toks = [normed] + [from_x(normed, j) for j in (1, 2, 3)]

    es = [e0] + [from_z(e0, k) for k in (1, 2, 3)]
    es = es + [from_core(e) for e in es]
    e_off = jnp.stack(
        [(((z + k) % NZ) * NC + c) * eighth for k in range(NZ)]
        + [(((z + k) % NZ) * NC + (1 - c)) * eighth for k in range(NZ)]
    ).astype(I32)
    h_off = jnp.stack([c * half, (1 - c) * half] * 2).astype(I32)
    g1, g3 = from_core(h1), from_core(h3)

    w_own = packed(0, width)
    (u0,) = ffn(toks, [[w_own]], jnp.zeros((1,), I32), files, "ffn_own")
    (u2,) = ffn(toks, [es], e_off, files, "ffn_far")
    r2 = from_y(u2, NY - 2)
    u1, u3 = ffn(toks, [[h1, g1], [h3, g3]], h_off, files, "ffn_near")
    r1, r3 = from_y(u1, NY - 1), from_y(u3, NY - 3)
    pos = jnp.stack(
        [(((x + j) % NX) * NY + (y - k) % NY) * files for k in range(NY) for j in range(NX)]
    ).astype(I32)
    terms = down([u0, r1, r2, r3], w_down, pos, files)
    terms = lax.all_to_all(terms, "mp", 0, 0, tiled=True)
    emb = emb_of(terms, pooled_in, lengths.astype(F32)[:, None], files)

    k_total = cluster_slot.shape[0]
    owned = k_total // n_dp
    lookup = file_cluster[:, None] == jnp.arange(k_total, dtype=I32)[None, :]
    slot = jnp.sum(jnp.where(lookup, cluster_slot[None, :], 0), axis=1)
    owner, local = slot // owned, slot % owned + 1
    same = owner[:, None] == owner[None, :]
    earlier = jnp.arange(files, dtype=I32)[None, :] < jnp.arange(files, dtype=I32)[:, None]
    rank = jnp.sum((same & earlier).astype(I32), axis=1)
    place = (owner[None, None, :] == jnp.arange(n_dp, dtype=I32)[:, None, None]) & (
        rank[None, None, :] == jnp.arange(files, dtype=I32)[None, :, None]
    )
    send_lp = jnp.sum(jnp.where(place, local[None, None, :], 0), axis=2)
    send_ord = jnp.sum(jnp.where(place, file_order[None, None, :], 0), axis=2)
    most = jnp.broadcast_to(jnp.max(rank) + 1, (n_dp, 1)).astype(I32)
    meta = jnp.concatenate([send_lp, send_ord, most], axis=1)
    meta = jnp.broadcast_to(meta[:, None, :], (n_dp, n_mp, 2 * files + 1)).reshape(n_dp * n_mp, 2 * files + 1)
    meta, _ = lax.optimization_barrier((meta, e0))
    meta = lax.all_to_all(meta, ALL, 0, 0, tiled=True)
    got_lp, got_ord = meta[:, :files], meta[:, files:2 * files]
    rounds = (jnp.max(meta[:, 2 * files]) + 1) // 2

    def one_round(r, best, sums, counts):
        here = lax.dynamic_slice_in_dim(place, 2 * r, 2, 1)
        sel = jnp.broadcast_to(here[:, None], (n_dp, n_mp, 2, files)).reshape(-1, files).astype(BF)
        rows = lax.all_to_all(spread(emb, sel), ALL, 0, 0, tiled=True)
        lp = lax.dynamic_slice_in_dim(got_lp, 2 * r, 2, 1).reshape(-1)
        order = lax.dynamic_slice_in_dim(got_ord, 2 * r, 2, 1).reshape(-1)
        mine = lp == mp + 1
        member = jnp.broadcast_to(mine[None, :], (8, lp.shape[0])).astype(BF)
        top, new = match(rows, lp[:, None], order[:, None], member, bank, bank_slot, bank_order)
        back = lax.all_to_all(top.reshape(-1, 2), ALL, 0, 0, tiled=True)
        back = jnp.max(back.reshape(n_dp, n_mp, 2), axis=1)
        best = jnp.maximum(best, jnp.max(jnp.where(here, back[:, :, None], -1.0), axis=(0, 1)))
        return best, sums + new[:1], counts + jnp.sum(mine.astype(F32))

    state = one_round(0, jnp.full((files,), -1.0, F32), jnp.zeros((1, width), F32), jnp.float32(0))
    _, best, sums, counts = lax.while_loop(
        lambda s: s[0] < rounds, lambda s: (s[0] + 1,) + one_round(*s), (jnp.int32(1),) + state
    )
    centroid_new = (count_old[:, None] * centroid_old + sums) / (count_old + counts)[:, None]
    return best, centroid_new


def solution(mesh):
    both = P(ALL)
    rows = P(ALL, None)
    return jax.shard_map(
        on_device,
        mesh=mesh,
        in_specs=(
            rows, P(), P(None, "mp"), P(None, "mp"), P("mp", None), both, both, both, P(), rows, both, both, rows, both,
        ),
        out_specs=(both, rows),
        check_vma=False,
    )
```

```python
import functools

import jax
import jax.numpy as jnp
from jax import lax
from jax.experimental import pallas as pl
from jax.experimental.pallas import tpu as pltpu
from jax.sharding import PartitionSpec as P

ALL = ("dp", "mp")
NX, NY, NZ, NC = 4, 4, 4, 2
ORDERS = 1 << 20
BF, F32, I32 = jnp.bfloat16, jnp.float32, jnp.int32
VMEM = pltpu.CompilerParams(vmem_limit_bytes=56 * 1024 * 1024)
NT = (((1,), (1,)), ((), ()))


def from_x(v, j):
    perm = [(((x + j) % NX) * NY + y, x * NY + y) for x in range(NX) for y in range(NY)]
    return lax.ppermute(v, "mp", perm)


def from_y(v, k):
    perm = [(x * NY + (y + k) % NY, x * NY + y) for x in range(NX) for y in range(NY)]
    return lax.ppermute(v, "mp", perm)


def from_z(v, k):
    perm = [(((z + k) % NZ) * NC + c, z * NC + c) for z in range(NZ) for c in range(NC)]
    return lax.ppermute(v, "dp", perm)


def from_core(v):
    return lax.ppermute(v, "dp", [(d ^ 1, d) for d in range(NZ * NC)])


def block_ones(files, file_len, dtype):
    row = lax.broadcasted_iota(I32, (files, files * file_len), 0)
    col = lax.broadcasted_iota(I32, (files, files * file_len), 1)
    return jnp.where(col // file_len == row, 1.0, 0.0).astype(dtype)


def prep_kernel(file_len, h_ref, gain_ref, mask_ref, n_ref, p_ref):
    resid = h_ref[...].astype(F32)
    scale = lax.rsqrt(jnp.mean(resid * resid, axis=-1, keepdims=True) + 1e-05)
    normed = resid * scale * gain_ref[...].astype(F32)
    keep = mask_ref[...] > 0.5
    n_ref[...] = jnp.where(keep, normed, 0.0).astype(BF)
    files = p_ref.shape[0]
    valid = jnp.where(keep, resid, 0.0).astype(BF)
    p_ref[...] = jnp.dot(block_ones(files, file_len, BF), valid, preferred_element_type=F32)


def prep(hidden, gain, mask, files):
    tok, width = hidden.shape
    return pl.pallas_call(
        functools.partial(prep_kernel, tok // files),
        out_shape=(jax.ShapeDtypeStruct((tok, width), BF), jax.ShapeDtypeStruct((files, width), F32)),
        compiler_params=VMEM,
        name="prep",
    )(hidden, gain[None, :], mask)


def ffn_kernel(n_tok, slice_parts, files, file_len, off_ref, *refs):
    toks, refs = refs[:n_tok], refs[n_tok:]
    n_parts = sum(slice_parts)
    parts, refs = refs[:n_parts], refs[n_parts:]
    outs, refs = refs[:len(slice_parts)], refs[len(slice_parts):]
    t_buf, w_buf, t_sem, w_sem = refs
    copies, at, row = [], 0, 0
    for s, count in enumerate(slice_parts):
        for p in range(at, at + count):
            cols = parts[p].shape[1]
            start = pl.multiple_of(off_ref[p], 128)
            copies.append(pltpu.make_async_copy(parts[p], w_buf.at[s, :, pl.ds(start, cols)], w_sem.at[p]))
            copies[-1].start()
        at += count
        if s == 0:
            t_copies = []
            for t in range(n_tok):
                rows = toks[t].shape[0]
                t_copies.append(pltpu.make_async_copy(toks[t], t_buf.at[pl.ds(row, rows)], t_sem.at[t]))
                t_copies[-1].start()
                row += rows
    n_rows = t_buf.shape[0]
    hid = w_buf.shape[1] // 2
    ones = block_ones(n_rows // file_len, file_len, BF)
    at = 0
    for s, count in enumerate(slice_parts):
        if s == 0:
            for cp in t_copies:
                cp.wait()
        for cp in copies[at:at + count]:
            cp.wait()
        at += count
        both = lax.dot_general(w_buf[s], t_buf[...], NT, preferred_element_type=F32)
        gate = both[:hid]
        units = (0.5 * gate * (1.0 + jnp.tanh(0.5 * gate)) * both[hid:]).astype(BF)
        outs[s][...] = lax.dot_general(ones, units, NT, preferred_element_type=F32)


def ffn(toks, slices, offs, file_len, name):
    n_tok = len(toks)
    width = toks[0].shape[1]
    n_rows = sum(t.shape[0] for t in toks)
    rows = slices[0][0].shape[0]
    flat = [p for s in slices for p in s]
    anyspec = pl.BlockSpec(memory_space=pl.ANY)
    out = jax.ShapeDtypeStruct((n_rows // file_len, rows // 2), F32)
    return pl.pallas_call(
        functools.partial(ffn_kernel, n_tok, tuple(len(s) for s in slices), n_rows // file_len, file_len),
        in_specs=[pl.BlockSpec(memory_space=pltpu.SMEM)] + [anyspec] * (n_tok + len(flat)),
        out_specs=tuple(pl.BlockSpec(memory_space=pltpu.VMEM) for _ in slices),
        out_shape=tuple(out for _ in slices),
        scratch_shapes=[
            pltpu.VMEM((n_rows, width), BF),
            pltpu.VMEM((len(slices), rows, width), BF),
            pltpu.SemaphoreType.DMA((n_tok,)),
            pltpu.SemaphoreType.DMA((len(flat),)),
        ],
        compiler_params=VMEM,
        name=name,
    )(offs, *toks, *flat)


def down_kernel(files, pos_ref, u0, u1, u2, u3, w_ref, o_ref, buf):
    for k, u in enumerate((u0, u1, u2, u3)):
        for j in range(NX):
            dst = pl.multiple_of(pos_ref[k * NX + j], files)
            buf[pl.ds(dst, files), :] = u[j * files:(j + 1) * files, :]
    rows = buf[...]
    hi = rows.astype(BF)
    lo = (rows - hi.astype(F32)).astype(BF)
    w = w_ref[...]
    o_ref[...] = jnp.dot(hi, w, preferred_element_type=F32) + jnp.dot(lo, w, preferred_element_type=F32)


def down(us, w_down, pos, files):
    rows = NX * NY * files
    vm = pl.BlockSpec(memory_space=pltpu.VMEM)
    return pl.pallas_call(
        functools.partial(down_kernel, files),
        in_specs=[pl.BlockSpec(memory_space=pltpu.SMEM)] + [vm] * 5,
        out_specs=vm,
        out_shape=jax.ShapeDtypeStruct((rows, w_down.shape[1]), F32),
        scratch_shapes=[pltpu.VMEM((rows, us[0].shape[1]), F32)],
        compiler_params=VMEM,
        name="down",
    )(pos, *us, w_down)


def emb_kernel(files, copies, t_ref, p_ref, len_ref, sel_ref, o_ref):
    total = p_ref[...]
    for m in range(t_ref.shape[0] // files):
        total = total + t_ref[m * files:(m + 1) * files, :]
    pooled = total / len_ref[...]
    norm = lax.rsqrt(jnp.sum(pooled * pooled, axis=-1, keepdims=True) + 1e-06)
    emb = (pooled * norm).astype(BF)
    rows = jnp.dot(sel_ref[...], emb, preferred_element_type=F32)
    for d in range(sel_ref.shape[0] // 2):
        pair = rows[2 * d:2 * d + 2, :].astype(BF)
        for m in range(copies):
            o_ref[d * copies + m] = pair


def emb_to_owners(terms, pooled, lens, sel, files, copies):
    return pl.pallas_call(
        functools.partial(emb_kernel, files, copies),
        out_shape=jax.ShapeDtypeStruct((sel.shape[0] // 2 * copies, 2, pooled.shape[1]), BF),
        compiler_params=VMEM,
        name="emb",
    )(terms, pooled, lens, sel)


def match_kernel(rows_ref, low_ref, high_ref, mem_ref, bank_ref, key_ref, best_ref, sums_ref):
    step = pl.program_id(0)

    @pl.when(step == 0)
    def _():
        best_ref[...] = jnp.full(best_ref.shape, -1.0, F32)
        sums_ref[...] = jnp.dot(mem_ref[...], rows_ref[...], preferred_element_type=F32)

    sims = lax.dot_general(bank_ref[...], rows_ref[...], NT, preferred_element_type=F32)
    key = key_ref[...]
    valid = (key >= low_ref[...]) & (key < high_ref[...])
    top = jnp.max(jnp.where(valid, sims, -1.0), axis=0, keepdims=True)
    best_ref[...] = jnp.maximum(best_ref[...], top)


def match(rows, low, high, member, bank, key):
    n, width = rows.shape
    block = 512
    whole = lambda shape: pl.BlockSpec(shape, lambda i: (0, 0))
    return pl.pallas_call(
        match_kernel,
        grid=(bank.shape[0] // block,),
        in_specs=[
            whole((n, width)),
            whole((1, n)),
            whole((1, n)),
            whole(member.shape),
            pl.BlockSpec((block, width), lambda i: (i, 0)),
            pl.BlockSpec((block, 1), lambda i: (i, 0)),
        ],
        out_specs=(whole((1, n)), whole((member.shape[0], width))),
        out_shape=(jax.ShapeDtypeStruct((1, n), F32), jax.ShapeDtypeStruct((member.shape[0], width), F32)),
        compiler_params=VMEM,
        name="match",
    )(rows, low, high, member, bank, key)


def on_device(
    hidden_in,
    mlp_gain,
    w_gate,
    w_up,
    w_down,
    lengths,
    file_cluster,
    file_order,
    cluster_slot,
    bank,
    bank_slot,
    bank_order,
    centroid_old,
    count_old,
):
    tok, width = hidden_in.shape
    files = lengths.shape[0]
    file_len = tok // files
    n_dp, n_mp = NZ * NC, NX * NY
    dp, mp = lax.axis_index("dp"), lax.axis_index("mp")
    z, c, x, y = dp // NC, dp % NC, mp // NY, mp % NY
    tie = lax.optimization_barrier

    k_total = cluster_slot.shape[0]
    owned = k_total // n_dp
    lookup = file_cluster[:, None] == jnp.arange(k_total, dtype=I32)[None, :]
    slot = jnp.sum(jnp.where(lookup, cluster_slot[None, :], 0), axis=1)
    owner = slot // owned
    ids = jnp.arange(files, dtype=I32)
    rank = jnp.sum(((owner[:, None] == owner[None, :]) & (ids[None, :] < ids[:, None])).astype(I32), axis=1)
    place = (owner[None, None, :] == jnp.arange(n_dp, dtype=I32)[:, None, None]) & (
        rank[None, None, :] == ids[None, :, None]
    )
    first = slot % owned * ORDERS
    send_low = jnp.sum(jnp.where(place, first[None, None, :] + 1, 0), axis=2) - 1
    send_high = jnp.sum(jnp.where(place, (first + file_order)[None, None, :] + 1, 0), axis=2) - 1
    most = jnp.broadcast_to(jnp.max(rank) + 1, (n_dp, 1)).astype(I32)
    meta = jnp.concatenate([send_low, send_high, most], axis=1)
    meta = jnp.broadcast_to(meta[:, None, :], (n_dp, n_mp, 2 * files + 1)).reshape(n_dp * n_mp, 2 * files + 1)
    bank_key = (bank_slot * ORDERS + bank_order)[:, None]

    eighth, half = width // 8, width // 2
    w_t = [w_gate.T, w_up.T]
    cut = lambda start, n: jnp.concatenate([lax.dynamic_slice_in_dim(w, start, n, 1) for w in w_t], axis=0)
    w_own = jnp.concatenate(w_t, axis=0)
    w_e, w_h = cut(dp * eighth, eighth), cut(c * half, half)
    mask = (jnp.arange(file_len, dtype=I32)[None, :] < lengths[:, None]).astype(F32).reshape(tok, 1)
    normed, pooled_in = prep(hidden_in, mlp_gain, mask, files)
    w_e, w_h, normed = tie((w_e, w_h, normed))

    e0 = from_y(w_e, 2)
    t1, t3 = from_x(normed, 1), from_x(normed, 3)
    h1, h3 = from_y(w_h, 1), from_y(w_h, 3)
    meta, e0 = tie((meta, e0))
    meta = lax.all_to_all(meta, ALL, 0, 0, tiled=True)
    es = [e0] + [from_z(e0, k) for k in (1, 2, 3)]
    es = es + [from_core(e) for e in es]
    t2a, t2b = from_x(t1[:tok // 2], 1), from_x(t3[tok // 2:], 3)
    toks = [normed, t1, t2a, t2b, t3]

    e_off = jnp.stack(
        [(((z + k) % NZ) * NC + c) * eighth for k in range(NZ)]
        + [(((z + k) % NZ) * NC + (1 - c)) * eighth for k in range(NZ)]
    ).astype(I32)
    h_off = jnp.stack([c * half, (1 - c) * half] * 2).astype(I32)
    pos = jnp.stack(
        [(((x + j) % NX) * NY + (y - k) % NY) * files for k in range(NY) for j in range(NX)]
    ).astype(I32)
    lens = lengths.astype(F32)[:, None]
    got_low, got_high = meta[:, :files], meta[:, files:2 * files]
    rounds = (jnp.max(meta[:, 2 * files]) + 1) // 2

    def files_of(r):
        here = lax.dynamic_slice_in_dim(place, 2 * r, 2, 1)
        low = lax.dynamic_slice_in_dim(got_low, 2 * r, 2, 1).reshape(1, -1)
        high = lax.dynamic_slice_in_dim(got_high, 2 * r, 2, 1).reshape(1, -1)
        mine = low // ORDERS == mp
        mine = mine & (low >= 0)
        member = jnp.broadcast_to(mine, (8, low.shape[1])).astype(BF)
        return here.reshape(-1, files).astype(BF), here, low, high, member, jnp.sum(mine.astype(F32))

    ready = files_of(0)
    normed, e_off, h_off, pos, lens, rounds, bank_key, ready = tie(
        (normed, e_off, h_off, pos, lens, rounds, bank_key, ready)
    )
    toks[0] = normed

    (u0,) = ffn(toks, [[w_own]], jnp.zeros((1,), I32), file_len, "ffn_own")
    (u2,) = ffn(toks, [es], e_off, file_len, "ffn_far")
    h1, h3, u0, u2 = tie((h1, h3, u0, u2))
    g1, g3 = from_core(h1), from_core(h3)
    r2 = from_y(u2, NY - 2)
    u1, u3 = ffn(toks, [[h1, g1], [h3, g3]], h_off, file_len, "ffn_near")
    r1, r3 = from_y(u1, NY - 1), from_y(u3, NY - 3)
    terms = down([u0, r1, r2, r3], w_down, pos, files)
    terms = lax.all_to_all(terms, "mp", 0, 0, tiled=True)

    def one_round(ready, best, sums, counts):
        sel, here, low, high, member, count = ready
        rows = emb_to_owners(terms, pooled_in, lens, sel, files, n_mp)
        rows = lax.all_to_all(rows, ALL, 0, 0, tiled=True).reshape(-1, width)
        top, new = match(rows, low, high, member, bank, bank_key)
        back = lax.all_to_all(top.reshape(-1, 2), ALL, 0, 0, tiled=True)
        back = jnp.max(back.reshape(n_dp, n_mp, 2), axis=1)
        best = jnp.maximum(best, jnp.max(jnp.where(here, back[:, :, None], -1.0), axis=(0, 1)))
        return best, sums + new[:1], counts + count

    state = one_round(ready, jnp.full((files,), -1.0, F32), jnp.zeros((1, width), F32), jnp.float32(0))
    _, best, sums, counts = lax.while_loop(
        lambda s: s[0] < rounds,
        lambda s: (s[0] + 1,) + one_round(files_of(s[0]), *s[1:]),
        (jnp.int32(1),) + state,
    )
    centroid_new = (count_old[:, None] * centroid_old + sums) / (count_old + counts)[:, None]
    return best, centroid_new


def solution(mesh):
    both = P(ALL)
    rows = P(ALL, None)
    return jax.shard_map(
        on_device,
        mesh=mesh,
        in_specs=(
            rows, P(), P(None, "mp"), P(None, "mp"), P("mp", None), both, both, both, P(), rows, both, both, rows, both,
        ),
        out_specs=(both, rows),
        check_vma=False,
    )
```

```python
import functools

import jax
import jax.numpy as jnp
from jax import lax
from jax.experimental import pallas as pl
from jax.experimental.pallas import tpu as pltpu
from jax.sharding import PartitionSpec as P

ALL = ("dp", "mp")
NX, NY, NZ, NC = 4, 4, 4, 2
ORDERS = 1 << 20
BF, F32, I32 = jnp.bfloat16, jnp.float32, jnp.int32
VMEM = pltpu.CompilerParams(vmem_limit_bytes=56 * 1024 * 1024)
NT = (((1,), (1,)), ((), ()))


def from_x(v, j):
    perm = [(((x + j) % NX) * NY + y, x * NY + y) for x in range(NX) for y in range(NY)]
    return lax.ppermute(v, "mp", perm)


def from_y(v, k):
    perm = [(x * NY + (y + k) % NY, x * NY + y) for x in range(NX) for y in range(NY)]
    return lax.ppermute(v, "mp", perm)


def from_core(v):
    return lax.ppermute(v, "dp", [(d ^ 1, d) for d in range(NZ * NC)])


def block_ones(files, file_len, dtype):
    row = lax.broadcasted_iota(I32, (files, files * file_len), 0)
    col = lax.broadcasted_iota(I32, (files, files * file_len), 1)
    return jnp.where(col // file_len == row, 1.0, 0.0).astype(dtype)


def prep_kernel(file_len, len_ref, h_ref, gain_ref, n_ref, p_ref):
    gain = gain_ref[...].astype(F32)
    ones = jnp.ones((p_ref.shape[0], file_len), BF)
    for f in range(p_ref.shape[0]):
        rows = slice(f * file_len, (f + 1) * file_len)
        raw = h_ref[rows, :]
        resid = raw.astype(F32)
        scale = lax.rsqrt(jnp.mean(resid * resid, axis=-1, keepdims=True) + 1e-05)
        keep = lax.broadcasted_iota(I32, (file_len, 1), 0) < len_ref[f]
        n_ref[rows, :] = jnp.where(keep, resid * scale * gain, 0.0).astype(BF)
        valid = jnp.where(keep, resid, 0.0).astype(BF)
        p_ref[f:f + 1, :] = jnp.dot(ones, valid, preferred_element_type=F32)[:1]


def prep(hidden, gain, lengths):
    tok, width = hidden.shape
    files = lengths.shape[0]
    vm = pl.BlockSpec(memory_space=pltpu.VMEM)
    return pl.pallas_call(
        functools.partial(prep_kernel, tok // files),
        in_specs=[pl.BlockSpec(memory_space=pltpu.SMEM), vm, vm],
        out_specs=(vm, vm),
        out_shape=(jax.ShapeDtypeStruct((tok, width), BF), jax.ShapeDtypeStruct((files, width), F32)),
        compiler_params=pltpu.CompilerParams(vmem_limit_bytes=16 * 1024 * 1024),
        name="prep",
    )(lengths, hidden, gain[None, :])


def ffn_kernel(slice_parts, n_tok, n_old, file_len, off_ref, *refs):
    toks, refs = refs[:n_tok], refs[n_tok:]
    n_parts = sum(slice_parts)
    parts, refs = refs[:n_parts], refs[n_parts:]
    olds, refs = refs[:n_old], refs[n_old:]
    outs, bufs = refs[:len(slice_parts)], refs[len(slice_parts):]
    at = 0
    for s, count in enumerate(slice_parts):
        mine = parts[at:at + count]
        cols = mine[0].shape[-1]
        offs = [pl.multiple_of(off_ref[at + p], 128) for p in range(count)]
        at += count
        hid = mine[0].shape[-2] // 2
        row = 0
        if n_old:
            row = olds[s].shape[0]
            outs[s][:row, :] = olds[s][...]
        if len(mine[0].shape) == 3:
            for part, off in zip(mine, offs):
                for q in range(part.shape[0]):
                    bufs[0][:, pl.ds(off + q * count * cols, cols)] = part[q]
            mine, offs, cols = [bufs[0]], [0], bufs[0].shape[1]
        for t in toks:
            both = None
            for w, off in zip(mine, offs):
                x = t[...] if len(mine) == 1 else t[:, pl.ds(off, cols)]
                term = lax.dot_general(w[...], x, NT, preferred_element_type=F32)
                both = term if both is None else both + term
            gate = both[:hid]
            units = (0.5 * gate * (1.0 + jnp.tanh(0.5 * gate)) * both[hid:]).astype(BF)
            n = t.shape[0] // file_len
            ones = block_ones(n, file_len, BF)
            outs[s][row:row + n, :] = lax.dot_general(ones, units, NT, preferred_element_type=F32)
            row += n


def ffn(toks, slices, offs, file_len, name, olds=()):
    width = toks[0].shape[1]
    n_files = sum(t.shape[0] for t in toks) // file_len + (olds[0].shape[0] if olds else 0)
    rows = slices[0][0].shape[-2]
    flat = [p for s in slices for p in s]
    vm = pl.BlockSpec(memory_space=pltpu.VMEM)
    return pl.pallas_call(
        functools.partial(ffn_kernel, tuple(len(s) for s in slices), len(toks), len(olds), file_len),
        in_specs=[pl.BlockSpec(memory_space=pltpu.SMEM)] + [vm] * (len(toks) + len(flat) + len(olds)),
        out_specs=tuple(vm for _ in slices),
        out_shape=tuple(jax.ShapeDtypeStruct((n_files, rows // 2), F32) for _ in slices),
        scratch_shapes=[pltpu.VMEM((rows, width), BF)] if max(p.ndim for p in flat) > 2 else [],
        compiler_params=pltpu.CompilerParams(vmem_limit_bytes=24 * 1024 * 1024),
        name=name,
    )(offs, *toks, *flat, *olds)


def down_kernel(files, pos_ref, u0, u1, u2, u3, w_ref, o_ref, buf):
    for k, u in enumerate((u0, u1, u2, u3)):
        for j in range(NX):
            dst = pl.multiple_of(pos_ref[k * NX + j], files)
            buf[pl.ds(dst, files), :] = u[j * files:(j + 1) * files, :]
    rows = buf[...]
    hi = rows.astype(BF)
    lo = (rows - hi.astype(F32)).astype(BF)
    w = w_ref[...]
    o_ref[...] = jnp.dot(hi, w, preferred_element_type=F32) + jnp.dot(lo, w, preferred_element_type=F32)


def down(us, w_down, pos, files):
    rows = NX * NY * files
    vm = pl.BlockSpec(memory_space=pltpu.VMEM)
    return pl.pallas_call(
        functools.partial(down_kernel, files),
        in_specs=[pl.BlockSpec(memory_space=pltpu.SMEM)] + [vm] * 5,
        out_specs=vm,
        out_shape=jax.ShapeDtypeStruct((rows, w_down.shape[1]), F32),
        scratch_shapes=[pltpu.VMEM((rows, us[0].shape[1]), F32)],
        compiler_params=VMEM,
        name="down",
    )(pos, *us, w_down)


def emb_kernel(files, copies, t_ref, p_ref, len_ref, sel_ref, meta_ref, o_ref):
    total = p_ref[...]
    for m in range(t_ref.shape[0] // files):
        total = total + t_ref[m * files:(m + 1) * files, :]
    pooled = total / len_ref[...]
    norm = lax.rsqrt(jnp.sum(pooled * pooled, axis=-1, keepdims=True) + 1e-06)
    emb = (pooled * norm).astype(BF)
    width = emb.shape[1]
    rows = jnp.dot(sel_ref[...], emb, preferred_element_type=F32)
    for d in range(sel_ref.shape[0] // 2):
        pair = rows[2 * d:2 * d + 2, :].astype(BF)
        about = meta_ref[2 * d:2 * d + 2, :].astype(BF)
        for m in range(copies):
            o_ref[d * copies + m, :, :width] = pair
            o_ref[d * copies + m, :, width:] = about


def emb_to_owners(terms, pooled, lens, sel, meta, files, copies):
    return pl.pallas_call(
        functools.partial(emb_kernel, files, copies),
        out_shape=jax.ShapeDtypeStruct((sel.shape[0] // 2 * copies, 2, pooled.shape[1] + meta.shape[1]), BF),
        compiler_params=pltpu.CompilerParams(vmem_limit_bytes=16 * 1024 * 1024),
        name="emb",
    )(terms, pooled, lens, sel, meta)


def match_kernel(mp_ref, rows_ref, bank_ref, key_ref, best_ref, sums_ref, about_ref):
    width = bank_ref.shape[1]
    rows = rows_ref[:, :width]
    pick = lax.broadcasted_iota(I32, (8, 128), 0) == lax.broadcasted_iota(I32, (8, 128), 1)
    digits = lax.dot_general(
        jnp.where(pick, 1.0, 0.0).astype(BF), rows_ref[:, width:], NT, preferred_element_type=F32
    )
    low = digits[0:1] * 65536.0 + digits[1:2] * 256.0 + digits[2:3]
    high = digits[3:4] * 65536.0 + digits[4:5] * 256.0 + digits[5:6]
    mine = digits[6:7] == (mp_ref[0] + 1).astype(F32)
    member = jnp.broadcast_to(jnp.where(mine, 1.0, 0.0), (8, rows.shape[0])).astype(BF)
    best = jnp.full((1, rows.shape[0]), -1.0, F32)
    block = 512
    for i in range(bank_ref.shape[0] // block):
        at = slice(i * block, (i + 1) * block)
        sims = lax.dot_general(bank_ref[at, :], rows, NT, preferred_element_type=F32)
        key = key_ref[at, :]
        valid = (key >= low) & (key < high)
        best = jnp.maximum(best, jnp.max(jnp.where(valid, sims, -1.0), axis=0, keepdims=True))
    best_ref[...] = best
    sums_ref[...] = jnp.dot(member, rows, preferred_element_type=F32)
    count = jnp.sum(jnp.where(mine, 1.0, 0.0), axis=1, keepdims=True)
    most = jnp.max(digits[7:8], axis=1, keepdims=True)
    lane = lax.broadcasted_iota(I32, (1, 128), 1)
    about_ref[...] = jnp.where(lane == 0, count, most)


def match(rows, mp, bank, key):
    n = rows.shape[0]
    vm = pl.BlockSpec(memory_space=pltpu.VMEM)
    return pl.pallas_call(
        match_kernel,
        in_specs=[pl.BlockSpec(memory_space=pltpu.SMEM)] + [vm] * 3,
        out_specs=(vm, vm, vm),
        out_shape=(
            jax.ShapeDtypeStruct((1, n), F32),
            jax.ShapeDtypeStruct((8, bank.shape[1]), F32),
            jax.ShapeDtypeStruct((1, 128), F32),
        ),
        compiler_params=pltpu.CompilerParams(vmem_limit_bytes=24 * 1024 * 1024),
        name="match",
    )(mp[None], rows, bank, key)


def on_device(
    hidden_in,
    mlp_gain,
    w_gate,
    w_up,
    w_down,
    lengths,
    file_cluster,
    file_order,
    cluster_slot,
    bank,
    bank_slot,
    bank_order,
    centroid_old,
    count_old,
):
    tok, width = hidden_in.shape
    files = lengths.shape[0]
    file_len = tok // files
    n_dp, n_mp = NZ * NC, NX * NY
    dp, mp = lax.axis_index("dp"), lax.axis_index("mp")
    z, c, x, y = dp // NC, dp % NC, mp // NY, mp % NY
    tie = lax.optimization_barrier

    k_total = cluster_slot.shape[0]
    owned = k_total // n_dp
    lookup = file_cluster[:, None] == jnp.arange(k_total, dtype=I32)[None, :]
    slot = jnp.sum(jnp.where(lookup, cluster_slot[None, :], 0), axis=1)
    owner = slot // owned
    ids = jnp.arange(files, dtype=I32)
    rank = jnp.sum(((owner[:, None] == owner[None, :]) & (ids[None, :] < ids[:, None])).astype(I32), axis=1)
    place = (owner[None, None, :] == jnp.arange(n_dp, dtype=I32)[:, None, None]) & (
        rank[None, None, :] == ids[None, :, None]
    )
    local = slot % owned
    first = local * ORDERS
    key = first + file_order
    bank_key = (bank_slot * ORDERS + bank_order).astype(F32)[:, None]
    low_key, high_key = [first >> 16, first * 0, first * 0], [key >> 16, (key >> 8) & 255, key & 255]
    digits = jnp.stack(low_key + high_key + [local + 1, jnp.broadcast_to(jnp.max(rank) + 1, slot.shape)], axis=1)

    def files_of(r):
        here = lax.dynamic_slice_in_dim(place, 2 * r, 2, 1)
        sel = here.reshape(-1, files)
        meta = jnp.sum(jnp.where(sel[:, :, None], digits[None], 0), axis=1).astype(F32)
        return here, sel.astype(BF), jnp.pad(meta, ((0, 0), (0, 120)))

    eighth, half = width // 8, width // 2
    w_t = [w_gate.T, w_up.T]
    cut = lambda start, n: jnp.concatenate([lax.dynamic_slice_in_dim(w, start, n, 1) for w in w_t], axis=0)
    w_own = jnp.concatenate(w_t, axis=0)
    w_e = cut(dp * eighth, eighth)
    w_e, hidden_in, w_t = tie((w_e, hidden_in, w_t))
    e0 = from_y(w_e, 2)
    w_h = cut(c * half, half)
    normed, pooled_in = prep(hidden_in, mlp_gain, lengths)
    w_h, normed, w_t = tie((w_h, normed, w_t))
    t1, t3 = from_x(normed, 1), from_x(normed, 3)
    h1, h3 = from_y(w_h, 1), from_y(w_h, 3)
    e0, normed = tie((e0, normed))
    column = [[z_ * NC + c_ for z_ in range(NZ)] for c_ in range(NC)]
    es = lax.all_to_all(jnp.broadcast_to(e0[None], (NZ,) + e0.shape), "dp", 0, 0, axis_index_groups=column, tiled=True)
    es, t1, t3 = tie((es, t1, t3))
    es = [es, from_core(es)]
    t2a, t2b = from_x(t1[:tok // 2], 1), from_x(t3[tok // 2:], 3)
    toks, last = [normed, t1, t3], [t2a, t2b]

    e_off = jnp.stack([c * eighth, (1 - c) * eighth]).astype(I32)
    h_off = jnp.stack([c * half, (1 - c) * half] * 2).astype(I32)
    pos = jnp.stack(
        [(((x + j) % NX) * NY + (y - k) % NY) * files for k in range(NY) for j in (0, 1, 3, 2)]
    ).astype(I32)
    lens = lengths.astype(F32)[:, None]
    ready = files_of(0)
    normed, e_off, h_off, pos, lens, bank_key, ready = tie((normed, e_off, h_off, pos, lens, bank_key, ready))
    toks[0] = normed

    zero = jnp.zeros((1,), I32)
    (u0,) = ffn(toks, [[w_own]], zero, file_len, "ffn_own")
    u0, es = tie((u0, es))
    (u2,) = ffn(toks + last, [es], e_off, file_len, "ffn_far")
    h1, h3, u2, last = tie((h1, h3, u2, last))
    (u0,) = ffn(last, [[w_own]], zero, file_len, "ffn_last", (u0,))
    g1, g3 = from_core(h1), from_core(h3)
    r2 = from_y(u2, NY - 2)
    u1, u3 = ffn(toks + last, [[h1, g1], [h3, g3]], h_off, file_len, "ffn_near")
    r1, r3 = from_y(u1, NY - 1), from_y(u3, NY - 3)
    terms = down([u0, r1, r2, r3], w_down, pos, files)
    terms = lax.all_to_all(terms, "mp", 0, 0, tiled=True)

    def one_round(ready, best, sums, counts):
        here, sel, meta = ready
        rows = emb_to_owners(terms, pooled_in, lens, sel, meta, files, n_mp)
        rows = lax.all_to_all(rows, ALL, 0, 0, tiled=True)
        top, new, about = match(rows.reshape(-1, rows.shape[2]), mp, bank, bank_key)
        back = lax.all_to_all(top.reshape(-1, 2), ALL, 0, 0, tiled=True)
        back = jnp.max(back.reshape(n_dp, n_mp, 2), axis=1)
        best = jnp.maximum(best, jnp.max(jnp.where(here, back[:, :, None], -1.0), axis=(0, 1)))
        return about[0, 1], (best, sums + new[:1], counts + about[0, 0])

    most, state = one_round(ready, jnp.full((files,), -1.0, F32), jnp.zeros((1, width), F32), jnp.float32(0))
    _, (best, sums, counts) = lax.while_loop(
        lambda s: 2 * s[0] < most.astype(I32),
        lambda s: (s[0] + 1, one_round(files_of(s[0]), *s[1])[1]),
        (jnp.int32(1), state),
    )
    centroid_new = (count_old[:, None] * centroid_old + sums) / (count_old + counts)[:, None]
    return best, centroid_new


def solution(mesh):
    both = P(ALL)
    rows = P(ALL, None)
    return jax.shard_map(
        on_device,
        mesh=mesh,
        in_specs=(
            rows, P(), P(None, "mp"), P(None, "mp"), P("mp", None), both, both, both, P(), rows, both, both, rows, both,
        ),
        out_specs=(both, rows),
        check_vma=False,
    )
```

```python
import functools

import jax
import jax.numpy as jnp
from jax import lax
from jax.experimental import pallas as pl
from jax.experimental.pallas import tpu as pltpu
from jax.sharding import PartitionSpec as P

ALL = ("dp", "mp")
NX, NY, NZ, NC = 4, 4, 4, 2
ORDERS = 1 << 20
BF, F32, I32 = jnp.bfloat16, jnp.float32, jnp.int32
NT = (((1,), (1,)), ((), ()))


def from_x(v, j):
    perm = [(((x + j) % NX) * NY + y, x * NY + y) for x in range(NX) for y in range(NY)]
    return lax.ppermute(v, "mp", perm)


def from_y(v, k):
    perm = [(x * NY + (y + k) % NY, x * NY + y) for x in range(NX) for y in range(NY)]
    return lax.ppermute(v, "mp", perm)


def from_z(v, other):
    return lax.ppermute(v, "dp", [(other[z] * NC + c, z * NC + c) for z in range(NZ) for c in range(NC)])


def from_core(v):
    return lax.ppermute(v, "dp", [(d ^ 1, d) for d in range(NZ * NC)])


def block_ones(files, file_len, dtype):
    row = lax.broadcasted_iota(I32, (files, files * file_len), 0)
    col = lax.broadcasted_iota(I32, (files, files * file_len), 1)
    return jnp.where(col // file_len == row, 1.0, 0.0).astype(dtype)


def prep_kernel(file_len, len_ref, h_ref, gain_ref, n_ref, p_ref):
    gain = gain_ref[...].astype(F32)
    ones = jnp.ones((p_ref.shape[0], file_len), BF)
    for f in range(p_ref.shape[0]):
        rows = slice(f * file_len, (f + 1) * file_len)
        raw = h_ref[rows, :]
        resid = raw.astype(F32)
        scale = lax.rsqrt(jnp.mean(resid * resid, axis=-1, keepdims=True) + 1e-05)
        keep = lax.broadcasted_iota(I32, (file_len, 1), 0) < len_ref[f]
        n_ref[rows, :] = jnp.where(keep, resid * scale * gain, 0.0).astype(BF)
        valid = jnp.where(keep, resid, 0.0).astype(BF)
        p_ref[f:f + 1, :] = jnp.dot(ones, valid, preferred_element_type=F32)[:1]


def prep(hidden, gain, lengths):
    tok, width = hidden.shape
    files = lengths.shape[0]
    vm = pl.BlockSpec(memory_space=pltpu.VMEM)
    return pl.pallas_call(
        functools.partial(prep_kernel, tok // files),
        in_specs=[pl.BlockSpec(memory_space=pltpu.SMEM), vm, vm],
        out_specs=(vm, vm),
        out_shape=(jax.ShapeDtypeStruct((tok, width), BF), jax.ShapeDtypeStruct((files, width), F32)),
        compiler_params=pltpu.CompilerParams(vmem_limit_bytes=16 * 1024 * 1024),
        name="prep",
    )(lengths, hidden, gain[None, :])


def ffn_kernel(plan, n_tok, file_len, off_ref, *refs):
    n_parts = sum(len(p) for p, _ in plan)
    n_old = sum(1 for _, first in plan if first)
    toks, refs = refs[:n_tok], refs[n_tok:]
    parts, refs = refs[:n_parts], refs[n_parts:]
    olds, refs = list(refs[:n_old]), refs[n_old:]
    outs, refs = refs[:len(plan)], refs[len(plan):]
    t_buf, w_buf, t_sem, w_sem = refs
    hid = w_buf.shape[1] // 2

    def load_tokens():
        row, done = 0, []
        for t in range(n_tok):
            rows = toks[t].shape[0]
            done.append(pltpu.make_async_copy(toks[t], t_buf.at[pl.ds(row, rows)], t_sem.at[t]))
            done[-1].start()
            row += rows
        return done

    at, sem, waits = 0, 0, []
    for s, (pieces, _) in enumerate(plan):
        mine = []
        for p, n in enumerate(pieces):
            ref = parts[at + p]
            cols = ref.shape[-1]
            for q in range(n):
                start = pl.multiple_of(off_ref[sem], 128)
                src = ref.at[q] if len(ref.shape) == 3 else ref
                mine.append(pltpu.make_async_copy(src, w_buf.at[s, :, pl.ds(start, cols)], w_sem.at[sem]))
                mine[-1].start()
                sem += 1
        at += len(pieces)
        waits.append(mine)
        if s == 0:
            t_waits = load_tokens()
    for cp in t_waits:
        cp.wait()
    for s, (_, first) in enumerate(plan):
        for cp in waits[s]:
            cp.wait()
        rows = t_buf.shape[0] - first
        both = lax.dot_general(w_buf[s], t_buf[first:, :], NT, preferred_element_type=F32)
        gate = both[:hid]
        units = (0.5 * gate * (1.0 + jnp.tanh(0.5 * gate)) * both[hid:]).astype(BF)
        ones = block_ones(rows // file_len, file_len, BF)
        new = lax.dot_general(ones, units, NT, preferred_element_type=F32)
        if first:
            outs[s][:first // file_len, :] = olds.pop(0)[...]
        outs[s][first // file_len:, :] = new


def ffn(toks, slices, firsts, offs, file_len, name, olds=()):
    width = toks[0].shape[1]
    n_rows = sum(t.shape[0] for t in toks)
    rows = slices[0][0].shape[-2]
    plan = tuple((tuple(p.shape[0] if p.ndim == 3 else 1 for p in s), f) for s, f in zip(slices, firsts))
    flat = [p for s in slices for p in s]
    vm, hbm = pl.BlockSpec(memory_space=pltpu.VMEM), pl.BlockSpec(memory_space=pl.ANY)
    return pl.pallas_call(
        functools.partial(ffn_kernel, plan, len(toks), file_len),
        in_specs=[pl.BlockSpec(memory_space=pltpu.SMEM)] + [hbm] * (len(toks) + len(flat)) + [vm] * len(olds),
        out_specs=tuple(vm for _ in slices),
        out_shape=tuple(jax.ShapeDtypeStruct((n_rows // file_len, rows // 2), F32) for _ in slices),
        scratch_shapes=[
            pltpu.VMEM((n_rows, width), BF),
            pltpu.VMEM((len(slices), rows, width), BF),
            pltpu.SemaphoreType.DMA((len(toks),)),
            pltpu.SemaphoreType.DMA((sum(sum(p) for p, _ in plan),)),
        ],
        compiler_params=pltpu.CompilerParams(vmem_limit_bytes=(16 + 4 * len(slices)) * 1024 * 1024),
        name=name,
    )(offs, *toks, *flat, *olds)


def down_kernel(files, pos_ref, u0, u1, u2, u3, w_ref, o_ref, buf):
    for k, u in enumerate((u0, u1, u2, u3)):
        for j in range(NX):
            dst = pl.multiple_of(pos_ref[k * NX + j], files)
            buf[pl.ds(dst, files), :] = u[j * files:(j + 1) * files, :]
    rows = buf[...]
    hi = rows.astype(BF)
    lo = (rows - hi.astype(F32)).astype(BF)
    w = w_ref[...]
    o_ref[...] = jnp.dot(hi, w, preferred_element_type=F32) + jnp.dot(lo, w, preferred_element_type=F32)


def down(us, w_down, pos, files):
    rows = NX * NY * files
    vm = pl.BlockSpec(memory_space=pltpu.VMEM)
    return pl.pallas_call(
        functools.partial(down_kernel, files),
        in_specs=[pl.BlockSpec(memory_space=pltpu.SMEM)] + [vm] * 5,
        out_specs=vm,
        out_shape=jax.ShapeDtypeStruct((rows, w_down.shape[1]), F32),
        scratch_shapes=[pltpu.VMEM((rows, us[0].shape[1]), F32)],
        compiler_params=pltpu.CompilerParams(vmem_limit_bytes=16 * 1024 * 1024),
        name="down",
    )(pos, *us, w_down)


def emb_kernel(files, copies, t_ref, p_ref, len_ref, sel_ref, meta_ref, o_ref):
    total = p_ref[...]
    for m in range(t_ref.shape[0] // files):
        total = total + t_ref[m * files:(m + 1) * files, :]
    pooled = total / len_ref[...]
    norm = lax.rsqrt(jnp.sum(pooled * pooled, axis=-1, keepdims=True) + 1e-06)
    emb = (pooled * norm).astype(BF)
    width = emb.shape[1]
    rows = jnp.dot(sel_ref[...], emb, preferred_element_type=F32)
    for d in range(sel_ref.shape[0] // 2):
        pair = rows[2 * d:2 * d + 2, :].astype(BF)
        about = meta_ref[2 * d:2 * d + 2, :].astype(BF)
        for m in range(copies):
            o_ref[d * copies + m, :, :width] = pair
            o_ref[d * copies + m, :, width:] = about


def emb_to_owners(terms, pooled, lens, sel, meta, files, copies):
    return pl.pallas_call(
        functools.partial(emb_kernel, files, copies),
        out_shape=jax.ShapeDtypeStruct((sel.shape[0] // 2 * copies, 2, pooled.shape[1] + meta.shape[1]), BF),
        compiler_params=pltpu.CompilerParams(vmem_limit_bytes=16 * 1024 * 1024),
        name="emb",
    )(terms, pooled, lens, sel, meta)


def match_kernel(mp_ref, rows_ref, bank_ref, key_ref, best_ref, sums_ref, about_ref, buf, sem):
    width = bank_ref.shape[1]
    n_blocks = sem.shape[0]
    block = bank_ref.shape[0] // n_blocks
    copies = []
    for i in range(n_blocks):
        at = pl.ds(i * block, block)
        copies.append(pltpu.make_async_copy(bank_ref.at[at], buf.at[at], sem.at[i]))
        copies[-1].start()
    rows = rows_ref[:, :width]
    n = rows.shape[0]
    pick = lax.broadcasted_iota(I32, (8, 128), 0) == lax.broadcasted_iota(I32, (8, 128), 1)
    digits = lax.dot_general(
        jnp.where(pick, 1.0, 0.0).astype(BF), rows_ref[:, width:], NT, preferred_element_type=F32
    )
    low = digits[0:1] * 65536.0 + digits[1:2] * 256.0 + digits[2:3]
    high = digits[3:4] * 65536.0 + digits[4:5] * 256.0 + digits[5:6]
    mine = digits[6:7] == (mp_ref[0] + 1).astype(F32)
    member = jnp.broadcast_to(jnp.where(mine, 1.0, 0.0), (8, n)).astype(BF)
    sums_ref[...] = jnp.dot(member, rows, preferred_element_type=F32)
    count = jnp.sum(jnp.where(mine, 1.0, 0.0), axis=1, keepdims=True)
    most = jnp.max(digits[7:8], axis=1, keepdims=True)
    about_ref[...] = jnp.where(lax.broadcasted_iota(I32, (1, 128), 1) == 0, count, most)
    best = jnp.full((1, n), -1.0, F32)
    for i in range(n_blocks):
        copies[i].wait()
        at = slice(i * block, (i + 1) * block)
        sims = lax.dot_general(buf[at, :], rows, NT, preferred_element_type=F32)
        key = key_ref[at, :]
        valid = (key >= low) & (key < high)
        best = jnp.maximum(best, jnp.max(jnp.where(valid, sims, -1.0), axis=0, keepdims=True))
    row = lax.broadcasted_iota(I32, (n // 2, n), 0)
    lane = lax.broadcasted_iota(I32, (n // 2, n), 1)
    best = jnp.broadcast_to(best, (n // 2, n))
    pair = [jnp.max(jnp.where(lane == 2 * row + i, best, -1.0), axis=1, keepdims=True) for i in (0, 1)]
    out_lane = lax.broadcasted_iota(I32, (n // 2, 128), 1)
    best_ref[:, 0, :] = jnp.where(out_lane == 0, pair[0], pair[1])


def match(rows, mp, bank, key):
    n = rows.shape[0]
    vm = pl.BlockSpec(memory_space=pltpu.VMEM)
    return pl.pallas_call(
        match_kernel,
        in_specs=[pl.BlockSpec(memory_space=pltpu.SMEM), vm, pl.BlockSpec(memory_space=pl.ANY), vm],
        out_specs=(vm, vm, vm),
        out_shape=(
            jax.ShapeDtypeStruct((n // 2, 1, 128), F32),
            jax.ShapeDtypeStruct((8, bank.shape[1]), F32),
            jax.ShapeDtypeStruct((1, 128), F32),
        ),
        scratch_shapes=[pltpu.VMEM(bank.shape, BF), pltpu.SemaphoreType.DMA((8,))],
        compiler_params=pltpu.CompilerParams(vmem_limit_bytes=24 * 1024 * 1024),
        name="match",
    )(mp[None], rows, bank, key)


def on_device(
    hidden_in,
    mlp_gain,
    w_gate,
    w_up,
    w_down,
    lengths,
    file_cluster,
    file_order,
    cluster_slot,
    bank,
    bank_slot,
    bank_order,
    centroid_old,
    count_old,
):
    tok, width = hidden_in.shape
    files = lengths.shape[0]
    file_len = tok // files
    n_dp, n_mp = NZ * NC, NX * NY
    dp, mp = lax.axis_index("dp"), lax.axis_index("mp")
    z, c, x, y = dp // NC, dp % NC, mp // NY, mp % NY
    tie = lax.optimization_barrier

    k_total = cluster_slot.shape[0]
    owned = k_total // n_dp
    lookup = file_cluster[:, None] == jnp.arange(k_total, dtype=I32)[None, :]
    slot = jnp.sum(jnp.where(lookup, cluster_slot[None, :], 0), axis=1)
    owner = slot // owned
    ids = jnp.arange(files, dtype=I32)
    rank = jnp.sum(((owner[:, None] == owner[None, :]) & (ids[None, :] < ids[:, None])).astype(I32), axis=1)
    place = (owner[None, None, :] == jnp.arange(n_dp, dtype=I32)[:, None, None]) & (
        rank[None, None, :] == ids[None, :, None]
    )
    local = slot % owned
    first = local * ORDERS
    key = first + file_order
    bank_key = (bank_slot * ORDERS + bank_order).astype(F32)[:, None]
    low_key, high_key = [first >> 16, first * 0, first * 0], [key >> 16, (key >> 8) & 255, key & 255]
    digits = jnp.stack(low_key + high_key + [local + 1, jnp.broadcast_to(jnp.max(rank) + 1, slot.shape)], axis=1)

    def files_of(r):
        here = lax.dynamic_slice_in_dim(place, 2 * r, 2, 1)
        sel = here.reshape(-1, files)
        meta = jnp.sum(jnp.where(sel[:, :, None], digits[None], 0), axis=1).astype(F32)
        return here, sel.astype(BF), jnp.pad(meta, ((0, 0), (0, 120)))

    eighth, half = width // 8, width // 2
    w_t = [w_gate.T, w_up.T]
    cut = lambda start, n: jnp.concatenate([lax.dynamic_slice_in_dim(w, start, n, 1) for w in w_t], axis=0)
    w_own = jnp.concatenate(w_t, axis=0)
    w_e = cut(dp * eighth, eighth)
    w_e, hidden_in, w_t = tie((w_e, hidden_in, w_t))
    e0 = from_y(w_e, 2)
    w_h = cut(c * half, half)
    normed, pooled_in = prep(hidden_in, mlp_gain, lengths)
    w_h, normed, w_t = tie((w_h, normed, w_t))
    t1, t3 = from_x(normed, 1), from_x(normed, 3)
    h1, h3 = from_y(w_h, 1), from_y(w_h, 3)
    e0, normed = tie((e0, normed))
    e1 = from_z(e0, (1, 0, 3, 2))
    e01 = jnp.stack([e0, e1])
    es = jnp.concatenate([e01, from_z(e01, (3, 2, 1, 0))])
    t1, t3 = tie((t1, t3))
    es = [es, from_core(es)]
    t2a, t2b = from_x(t1[:tok // 2], 1), from_x(t3[tok // 2:], 3)
    toks, last = [normed, t1, t3], [t2a, t2b]

    held = [z, z ^ 1, 3 - z, (3 - z) ^ 1]
    e_off = jnp.stack([(q * NC + k) * eighth for k in (c, 1 - c) for q in held]).astype(I32)
    h_off = jnp.stack([c * half, (1 - c) * half] * 2).astype(I32)
    pos = jnp.stack(
        [(((x + j) % NX) * NY + (y - k) % NY) * files for k in range(NY) for j in (0, 1, 3, 2)]
    ).astype(I32)
    lens = lengths.astype(F32)[:, None]
    ready = files_of(0)
    normed, e_off, h_off, pos, lens, bank_key, ready = tie((normed, e_off, h_off, pos, lens, bank_key, ready))
    toks[0] = normed

    zero = jnp.zeros((1,), I32)
    (u0,) = ffn(toks, [[w_own]], (0,), zero, file_len, "ffn_own")
    u0, es = tie((u0, es))
    (u2,) = ffn(toks, [es], (0,), e_off, file_len, "ffn_far")
    h1, h3, u2, last = tie((h1, h3, u2, last))
    g1, g3 = from_core(h1), from_core(h3)
    first = sum(t.shape[0] for t in toks)
    u2, u0, u1, u3 = ffn(
        toks + last,
        [es, [w_own], [h1, g1], [h3, g3]],
        (first, first, 0, 0),
        jnp.concatenate([e_off, zero, h_off]),
        file_len,
        "ffn_last",
        (u2, u0),
    )
    r2 = from_y(u2, NY - 2)
    r1, r3 = from_y(u1, NY - 1), from_y(u3, NY - 3)
    terms = down([u0, r1, r2, r3], w_down, pos, files)
    terms = lax.all_to_all(terms, "mp", 0, 0, tiled=True)

    def one_round(ready, best, sums, counts):
        here, sel, meta = ready
        rows = emb_to_owners(terms, pooled_in, lens, sel, meta, files, n_mp)
        rows = lax.all_to_all(rows, ALL, 0, 0, tiled=True)
        top, new, about = match(rows.reshape(-1, rows.shape[2]), mp, bank, bank_key)
        back = lax.all_to_all(top, ALL, 0, 0, tiled=True)
        back = jnp.max(back.reshape(n_dp, n_mp, -1), axis=1)[:, :2]
        best = jnp.maximum(best, jnp.max(jnp.where(here, back[:, :, None], -1.0), axis=(0, 1)))
        return about[0, 1], (best, sums + new[:1], counts + about[0, 0])

    most, state = one_round(ready, jnp.full((files,), -1.0, F32), jnp.zeros((1, width), F32), jnp.float32(0))
    _, (best, sums, counts) = lax.while_loop(
        lambda s: 2 * s[0] < most.astype(I32),
        lambda s: (s[0] + 1, one_round(files_of(s[0]), *s[1])[1]),
        (jnp.int32(1), state),
    )
    centroid_new = (count_old[:, None] * centroid_old + sums) / (count_old + counts)[:, None]
    return best, centroid_new


def solution(mesh):
    both = P(ALL)
    rows = P(ALL, None)
    return jax.shard_map(
        on_device,
        mesh=mesh,
        in_specs=(
            rows, P(), P(None, "mp"), P(None, "mp"), P("mp", None), both, both, both, P(), rows, both, both, rows, both,
        ),
        out_specs=(both, rows),
        check_vma=False,
    )
```

```python
import functools

import jax
import jax.numpy as jnp
from jax import lax
from jax.experimental import pallas as pl
from jax.experimental.pallas import tpu as pltpu
from jax.sharding import PartitionSpec as P

ALL = ("dp", "mp")
NX, NY, NZ, NC = 4, 4, 4, 2
ORDERS = 1 << 20
BF, F32, I32 = jnp.bfloat16, jnp.float32, jnp.int32
NT = (((1,), (1,)), ((), ()))


def from_x(v, j):
    perm = [(((x + j) % NX) * NY + y, x * NY + y) for x in range(NX) for y in range(NY)]
    return lax.ppermute(v, "mp", perm)


def from_y(v, k):
    perm = [(x * NY + (y + k) % NY, x * NY + y) for x in range(NX) for y in range(NY)]
    return lax.ppermute(v, "mp", perm)


def from_core(v):
    return lax.ppermute(v, "dp", [(d ^ 1, d) for d in range(NZ * NC)])


def block_ones(files, file_len, dtype):
    row = lax.broadcasted_iota(I32, (files, files * file_len), 0)
    col = lax.broadcasted_iota(I32, (files, files * file_len), 1)
    return jnp.where(col // file_len == row, 1.0, 0.0).astype(dtype)


def prep_kernel(file_len, len_ref, h_ref, gain_ref, n_ref, p_ref):
    gain = gain_ref[...].astype(F32)
    ones = jnp.ones((p_ref.shape[0], file_len), BF)
    for f in range(p_ref.shape[0]):
        rows = slice(f * file_len, (f + 1) * file_len)
        raw = h_ref[rows, :]
        resid = raw.astype(F32)
        scale = lax.rsqrt(jnp.mean(resid * resid, axis=-1, keepdims=True) + 1e-05)
        keep = lax.broadcasted_iota(I32, (file_len, 1), 0) < len_ref[f]
        n_ref[rows, :] = jnp.where(keep, resid * scale * gain, 0.0).astype(BF)
        valid = jnp.where(keep, resid, 0.0).astype(BF)
        p_ref[f:f + 1, :] = jnp.dot(ones, valid, preferred_element_type=F32)[:1]


def prep(hidden, gain, lengths):
    tok, width = hidden.shape
    files = lengths.shape[0]
    vm = pl.BlockSpec(memory_space=pltpu.VMEM)
    return pl.pallas_call(
        functools.partial(prep_kernel, tok // files),
        in_specs=[pl.BlockSpec(memory_space=pltpu.SMEM), vm, vm],
        out_specs=(vm, vm),
        out_shape=(jax.ShapeDtypeStruct((tok, width), BF), jax.ShapeDtypeStruct((files, width), F32)),
        compiler_params=pltpu.CompilerParams(vmem_limit_bytes=16 * 1024 * 1024),
        name="prep",
    )(lengths, hidden, gain[None, :])


def ffn_kernel(plan, n_tok, file_len, off_ref, *refs):
    n_parts = sum(len(p) for p, _ in plan)
    n_old = sum(1 for _, first in plan if first)
    toks, refs = refs[:n_tok], refs[n_tok:]
    parts, refs = refs[:n_parts], refs[n_parts:]
    olds, refs = list(refs[:n_old]), refs[n_old:]
    outs, refs = refs[:len(plan)], refs[len(plan):]
    t_buf, w_buf, t_sem, w_sem = refs
    hid = w_buf.shape[1] // 2

    def load_tokens():
        row, done = 0, []
        for t in range(n_tok):
            rows = toks[t].shape[0]
            done.append(pltpu.make_async_copy(toks[t], t_buf.at[pl.ds(row, rows)], t_sem.at[t]))
            done[-1].start()
            row += rows
        return done

    at, sem, waits = 0, 0, []
    for s, (pieces, _) in enumerate(plan):
        mine = []
        for p, n in enumerate(pieces):
            ref = parts[at + p]
            cols = ref.shape[-1]
            for q in range(n):
                start = pl.multiple_of(off_ref[sem], 128)
                src = ref.at[q] if len(ref.shape) == 3 else ref
                mine.append(pltpu.make_async_copy(src, w_buf.at[s, :, pl.ds(start, cols)], w_sem.at[sem]))
                mine[-1].start()
                sem += 1
        at += len(pieces)
        waits.append(mine)
        if s == 0:
            t_waits = load_tokens()
    for cp in t_waits:
        cp.wait()
    ones = block_ones(t_buf.shape[0] // file_len, file_len, BF)
    for s, (_, first) in enumerate(plan):
        for cp in waits[s]:
            cp.wait()
        both = lax.dot_general(w_buf[s], t_buf[...], NT, preferred_element_type=F32)
        gate = both[:hid]
        units = (0.5 * gate * (1.0 + jnp.tanh(0.5 * gate)) * both[hid:]).astype(BF)
        new = lax.dot_general(ones, units, NT, preferred_element_type=F32)
        if first:
            outs[s][:first // file_len, :] = olds.pop(0)[...]
        outs[s][first // file_len:, :] = new


def ffn(toks, slices, firsts, offs, file_len, name, olds=()):
    width = toks[0].shape[1]
    n_rows = sum(t.shape[0] for t in toks)
    rows = slices[0][0].shape[-2]
    plan = tuple((tuple(p.shape[0] if p.ndim == 3 else 1 for p in s), f) for s, f in zip(slices, firsts))
    flat = [p for s in slices for p in s]
    vm, hbm = pl.BlockSpec(memory_space=pltpu.VMEM), pl.BlockSpec(memory_space=pl.ANY)
    return pl.pallas_call(
        functools.partial(ffn_kernel, plan, len(toks), file_len),
        in_specs=[pl.BlockSpec(memory_space=pltpu.SMEM)] + [hbm] * (len(toks) + len(flat)) + [vm] * len(olds),
        out_specs=tuple(vm for _ in slices),
        out_shape=tuple(jax.ShapeDtypeStruct(((n_rows + f) // file_len, rows // 2), F32) for f in firsts),
        scratch_shapes=[
            pltpu.VMEM((n_rows, width), BF),
            pltpu.VMEM((len(slices), rows, width), BF),
            pltpu.SemaphoreType.DMA((len(toks),)),
            pltpu.SemaphoreType.DMA((sum(sum(p) for p, _ in plan),)),
        ],
        compiler_params=pltpu.CompilerParams(vmem_limit_bytes=(16 + 4 * len(slices)) * 1024 * 1024),
        name=name,
    )(offs, *toks, *flat, *olds)


def down_kernel(files, pos_ref, u0, u1, u2, u3, w_ref, o_ref, buf):
    for k, u in enumerate((u0, u1, u2, u3)):
        for j in range(NX):
            dst = pl.multiple_of(pos_ref[k * NX + j], files)
            buf[pl.ds(dst, files), :] = u[j * files:(j + 1) * files, :]
    rows = buf[...]
    hi = rows.astype(BF)
    lo = (rows - hi.astype(F32)).astype(BF)
    w = w_ref[...]
    o_ref[...] = jnp.dot(hi, w, preferred_element_type=F32) + jnp.dot(lo, w, preferred_element_type=F32)


def down(us, w_down, pos, files):
    rows = NX * NY * files
    vm = pl.BlockSpec(memory_space=pltpu.VMEM)
    return pl.pallas_call(
        functools.partial(down_kernel, files),
        in_specs=[pl.BlockSpec(memory_space=pltpu.SMEM)] + [vm] * 5,
        out_specs=vm,
        out_shape=jax.ShapeDtypeStruct((rows, w_down.shape[1]), F32),
        scratch_shapes=[pltpu.VMEM((rows, us[0].shape[1]), F32)],
        compiler_params=pltpu.CompilerParams(vmem_limit_bytes=16 * 1024 * 1024),
        name="down",
    )(pos, *us, w_down)


def emb_kernel(files, copies, t_ref, p_ref, len_ref, sel_ref, meta_ref, o_ref):
    total = p_ref[...]
    for m in range(t_ref.shape[0] // files):
        total = total + t_ref[m * files:(m + 1) * files, :]
    pooled = total / len_ref[...]
    norm = lax.rsqrt(jnp.sum(pooled * pooled, axis=-1, keepdims=True) + 1e-06)
    emb = (pooled * norm).astype(BF)
    width = emb.shape[1]
    rows = jnp.dot(sel_ref[...], emb, preferred_element_type=F32)
    for d in range(sel_ref.shape[0] // 2):
        pair = rows[2 * d:2 * d + 2, :].astype(BF)
        about = meta_ref[2 * d:2 * d + 2, :].astype(BF)
        for m in range(copies):
            o_ref[d * copies + m, :, :width] = pair
            o_ref[d * copies + m, :, width:] = about


def emb_to_owners(terms, pooled, lens, sel, meta, files, copies):
    return pl.pallas_call(
        functools.partial(emb_kernel, files, copies),
        out_shape=jax.ShapeDtypeStruct((sel.shape[0] // 2 * copies, 2, pooled.shape[1] + meta.shape[1]), BF),
        compiler_params=pltpu.CompilerParams(vmem_limit_bytes=16 * 1024 * 1024),
        name="emb",
    )(terms, pooled, lens, sel, meta)


def match_kernel(mp_ref, rows_ref, bank_ref, key_ref, best_ref, sums_ref, about_ref, buf, sem):
    width = bank_ref.shape[1]
    n_blocks = sem.shape[0]
    block = bank_ref.shape[0] // n_blocks
    copies = []
    for i in range(n_blocks):
        at = pl.ds(i * block, block)
        copies.append(pltpu.make_async_copy(bank_ref.at[at], buf.at[at], sem.at[i]))
        copies[-1].start()
    rows = jnp.concatenate([rows_ref[:, 0, :width], rows_ref[:, 1, :width]], axis=0)
    about = jnp.concatenate([rows_ref[:, 0, width:], rows_ref[:, 1, width:]], axis=0)
    n = rows.shape[0]
    pick = lax.broadcasted_iota(I32, (8, 128), 0) == lax.broadcasted_iota(I32, (8, 128), 1)
    digits = lax.dot_general(jnp.where(pick, 1.0, 0.0).astype(BF), about, NT, preferred_element_type=F32)
    low = digits[0:1] * 65536.0 + digits[1:2] * 256.0 + digits[2:3]
    high = digits[3:4] * 65536.0 + digits[4:5] * 256.0 + digits[5:6]
    mine = digits[6:7] == (mp_ref[0] + 1).astype(F32)
    member = jnp.broadcast_to(jnp.where(mine, 1.0, 0.0), (8, n)).astype(BF)
    sums_ref[...] = jnp.dot(member, rows, preferred_element_type=F32)
    count = jnp.sum(jnp.where(mine, 1.0, 0.0), axis=1, keepdims=True)
    most = jnp.max(digits[7:8], axis=1, keepdims=True)
    about_ref[...] = jnp.where(lax.broadcasted_iota(I32, (1, 128), 1) == 0, count, most)
    best = jnp.full((1, n), -1.0, F32)
    block *= n_blocks // 2
    for i in range(2):
        for cp in copies[i * n_blocks // 2:(i + 1) * n_blocks // 2]:
            cp.wait()
        at = slice(i * block, (i + 1) * block)
        sims = lax.dot_general(buf[at, :], rows, NT, preferred_element_type=F32)
        key = key_ref[at, :]
        valid = (key >= low) & (key < high)
        best = jnp.maximum(best, jnp.max(jnp.where(valid, sims, -1.0), axis=0, keepdims=True))
    n //= 2
    eye = lax.broadcasted_iota(I32, (n, n), 0) == lax.broadcasted_iota(I32, (n, n), 1)
    pair = [
        jnp.max(jnp.where(eye, jnp.broadcast_to(best[:, i * n:(i + 1) * n], (n, n)), -1.0), axis=1, keepdims=True)
        for i in (0, 1)
    ]
    out_lane = lax.broadcasted_iota(I32, (n, 128), 1)
    best_ref[:, 0, :] = jnp.where(out_lane == 0, pair[0], pair[1])


def match(rows, mp, bank, key):
    vm = pl.BlockSpec(memory_space=pltpu.VMEM)
    return pl.pallas_call(
        match_kernel,
        in_specs=[pl.BlockSpec(memory_space=pltpu.SMEM), vm, pl.BlockSpec(memory_space=pl.ANY), vm],
        out_specs=(vm, vm, vm),
        out_shape=(
            jax.ShapeDtypeStruct((rows.shape[0], 1, 128), F32),
            jax.ShapeDtypeStruct((8, bank.shape[1]), F32),
            jax.ShapeDtypeStruct((1, 128), F32),
        ),
        scratch_shapes=[pltpu.VMEM(bank.shape, BF), pltpu.SemaphoreType.DMA((8,))],
        compiler_params=pltpu.CompilerParams(vmem_limit_bytes=24 * 1024 * 1024),
        name="match",
    )(mp[None], rows, bank, key)


def on_device(
    hidden_in,
    mlp_gain,
    w_gate,
    w_up,
    w_down,
    lengths,
    file_cluster,
    file_order,
    cluster_slot,
    bank,
    bank_slot,
    bank_order,
    centroid_old,
    count_old,
):
    tok, width = hidden_in.shape
    files = lengths.shape[0]
    file_len = tok // files
    n_dp, n_mp = NZ * NC, NX * NY
    dp, mp = lax.axis_index("dp"), lax.axis_index("mp")
    z, c, x, y = dp // NC, dp % NC, mp // NY, mp % NY
    tie = lax.optimization_barrier

    k_total = cluster_slot.shape[0]
    owned = k_total // n_dp
    lookup = file_cluster[:, None] == jnp.arange(k_total, dtype=I32)[None, :]
    slot = jnp.sum(jnp.where(lookup, cluster_slot[None, :], 0), axis=1)
    owner = slot // owned
    ids = jnp.arange(files, dtype=I32)
    rank = jnp.sum(((owner[:, None] == owner[None, :]) & (ids[None, :] < ids[:, None])).astype(I32), axis=1)
    place = (owner[None, None, :] == jnp.arange(n_dp, dtype=I32)[:, None, None]) & (
        rank[None, None, :] == ids[None, :, None]
    )
    local = slot % owned
    first = local * ORDERS
    key = first + file_order
    bank_key = (bank_slot * ORDERS + bank_order).astype(F32)[:, None]
    low_key, high_key = [first >> 16, first * 0, first * 0], [key >> 16, (key >> 8) & 255, key & 255]
    digits = jnp.stack(low_key + high_key + [local + 1, jnp.broadcast_to(jnp.max(rank) + 1, slot.shape)], axis=1)

    def files_of(r):
        here = lax.dynamic_slice_in_dim(place, 2 * r, 2, 1)
        sel = here.reshape(-1, files)
        meta = jnp.sum(jnp.where(sel[:, :, None], digits[None], 0), axis=1).astype(F32)
        return here, sel.astype(BF), jnp.pad(meta, ((0, 0), (0, 120)))

    half, quarter = width // 2, width // 4
    w_t = [w_gate.T, w_up.T]
    w_h = jnp.concatenate([lax.dynamic_slice_in_dim(w, c * half, half, 1) for w in w_t], axis=0)
    normed, pooled_in = prep(hidden_in, mlp_gain, lengths)
    w_h, normed, w_t = tie((w_h, normed, w_t))
    t1, t3 = from_x(normed, 1), from_x(normed, 3)
    h1, h3 = from_y(w_h, 1), from_y(w_h, 3)
    w_own = jnp.concatenate(w_t, axis=0)
    t1, t3 = tie((t1, t3))
    t2a, t2b = from_x(t1[:tok // 2], 1), from_x(t3[tok // 2:], 3)
    toks, last = [normed, t1, t3], [t2a, t2b]

    h_off = jnp.stack([c * half, (1 - c) * half]).astype(I32)
    e_off = jnp.stack([k * half + q * quarter for k in (c, 1 - c) for q in (0, 1)]).astype(I32)
    pos = jnp.stack(
        [(((x + j) % NX) * NY + (y - k) % NY) * files for k in range(NY) for j in (0, 1, 3, 2)]
    ).astype(I32)
    lens = lengths.astype(F32)[:, None]
    ready = files_of(0)
    normed, e_off, h_off, pos, lens, bank_key, ready = tie((normed, e_off, h_off, pos, lens, bank_key, ready))
    toks[0] = normed

    zero = jnp.zeros((1,), I32)
    (u0,) = ffn(toks, [[w_own]], (0,), zero, file_len, "ffn_own")
    h1, h3, u0 = tie((h1, h3, u0))
    k2a, k2b = from_y(h1[:, :quarter], 1), from_y(h3[:, quarter:], 3)
    near = [[h1, from_core(h1)], [h3, from_core(h3)]]
    near_off = jnp.concatenate([h_off, h_off])
    u1, u3 = ffn(toks, near, (0, 0), near_off, file_len, "ffn_near")
    first = sum(t.shape[0] for t in toks)
    u1, u3, last = tie((u1, u3, last))
    rest = jnp.concatenate([near_off, zero])
    u1, u3, u0 = ffn(last, near + [[w_own]], (first,) * 3, rest, file_len, "ffn_rest", (u1, u3, u0))
    r1, r3 = from_y(u1, NY - 1), from_y(u3, NY - 3)
    k2a, k2b, u0 = tie((k2a, k2b, u0))
    far = [k2a, k2b, from_core(k2a), from_core(k2b)]
    (u2,) = ffn(toks + last, [far], (0,), e_off, file_len, "ffn_far")
    r2 = from_y(u2, NY - 2)
    terms = down([u0, r1, r2, r3], w_down, pos, files)
    terms = lax.all_to_all(terms, "mp", 0, 0, tiled=True)

    def one_round(ready, best, sums, counts):
        here, sel, meta = ready
        rows = emb_to_owners(terms, pooled_in, lens, sel, meta, files, n_mp)
        rows = lax.all_to_all(rows, ALL, 0, 0, tiled=True)
        top, new, about = match(rows, mp, bank, bank_key)
        back = lax.all_to_all(top, ALL, 0, 0, tiled=True)
        back = jnp.max(back.reshape(n_dp, n_mp, -1), axis=1)[:, :2]
        best = jnp.maximum(best, jnp.max(jnp.where(here, back[:, :, None], -1.0), axis=(0, 1)))
        return about[0, 1], (best, sums + new[:1], counts + about[0, 0])

    most, state = one_round(ready, jnp.full((files,), -1.0, F32), jnp.zeros((1, width), F32), jnp.float32(0))
    _, (best, sums, counts) = lax.while_loop(
        lambda s: 2 * s[0] < most.astype(I32),
        lambda s: (s[0] + 1, one_round(files_of(s[0]), *s[1])[1]),
        (jnp.int32(1), state),
    )
    centroid_new = (count_old[:, None] * centroid_old + sums) / (count_old + counts)[:, None]
    return best, centroid_new


def solution(mesh):
    both = P(ALL)
    rows = P(ALL, None)
    return jax.shard_map(
        on_device,
        mesh=mesh,
        in_specs=(
            rows, P(), P(None, "mp"), P(None, "mp"), P("mp", None), both, both, both, P(), rows, both, both, rows, both,
        ),
        out_specs=(both, rows),
        check_vma=False,
    )
```

```python
import functools

import jax
import jax.numpy as jnp
from jax import lax
from jax.experimental import pallas as pl
from jax.experimental.pallas import tpu as pltpu
from jax.sharding import PartitionSpec as P

ALL = ("dp", "mp")
NX, NY, NZ, NC = 4, 4, 4, 2
ORDERS = 1 << 20
BF, F32, I32 = jnp.bfloat16, jnp.float32, jnp.int32
NT = (((1,), (1,)), ((), ()))


def from_x(v, j):
    perm = [(((x + j) % NX) * NY + y, x * NY + y) for x in range(NX) for y in range(NY)]
    return lax.ppermute(v, "mp", perm)


def from_y(v, k):
    perm = [(x * NY + (y + k) % NY, x * NY + y) for x in range(NX) for y in range(NY)]
    return lax.ppermute(v, "mp", perm)


def from_core(v):
    return lax.ppermute(v, "dp", [(d ^ 1, d) for d in range(NZ * NC)])


def block_ones(files, file_len, dtype):
    row = lax.broadcasted_iota(I32, (files, files * file_len), 0)
    col = lax.broadcasted_iota(I32, (files, files * file_len), 1)
    return jnp.where(col // file_len == row, 1.0, 0.0).astype(dtype)


def prep_kernel(file_len, len_ref, h_ref, gain_ref, n_ref, p_ref):
    gain = gain_ref[...].astype(F32)
    ones = jnp.ones((p_ref.shape[0], file_len), BF)
    for f in range(p_ref.shape[0]):
        rows = slice(f * file_len, (f + 1) * file_len)
        raw = h_ref[rows, :]
        resid = raw.astype(F32)
        scale = lax.rsqrt(jnp.mean(resid * resid, axis=-1, keepdims=True) + 1e-05)
        keep = lax.broadcasted_iota(I32, (file_len, 1), 0) < len_ref[f]
        n_ref[rows, :] = jnp.where(keep, resid * scale * gain, 0.0).astype(BF)
        valid = jnp.where(keep, resid, 0.0).astype(BF)
        p_ref[f:f + 1, :] = jnp.dot(ones, valid, preferred_element_type=F32)[:1]


def prep(hidden, gain, lengths):
    tok, width = hidden.shape
    files = lengths.shape[0]
    vm = pl.BlockSpec(memory_space=pltpu.VMEM)
    return pl.pallas_call(
        functools.partial(prep_kernel, tok // files),
        in_specs=[pl.BlockSpec(memory_space=pltpu.SMEM), vm, vm],
        out_specs=(vm, vm),
        out_shape=(jax.ShapeDtypeStruct((tok, width), BF), jax.ShapeDtypeStruct((files, width), F32)),
        compiler_params=pltpu.CompilerParams(vmem_limit_bytes=16 * 1024 * 1024),
        name="prep",
    )(lengths, hidden, gain[None, :])


def ffn_kernel(plan, n_tok, file_len, off_ref, *refs):
    n_parts = sum(len(p) for p, _ in plan)
    n_old = sum(1 for _, first in plan if first)
    toks, refs = refs[:n_tok], refs[n_tok:]
    parts, refs = refs[:n_parts], refs[n_parts:]
    olds, refs = list(refs[:n_old]), refs[n_old:]
    outs, refs = refs[:len(plan)], refs[len(plan):]
    t_buf, w_buf, t_sem, w_sem = refs
    hid = w_buf.shape[1] // 2

    def load_tokens():
        row, done = 0, []
        for t in range(n_tok):
            rows = toks[t].shape[0]
            done.append(pltpu.make_async_copy(toks[t], t_buf.at[pl.ds(row, rows)], t_sem.at[t]))
            done[-1].start()
            row += rows
        return done

    at, sem, waits = 0, 0, []
    for s, (pieces, _) in enumerate(plan):
        mine = []
        for p, n in enumerate(pieces):
            ref = parts[at + p]
            cols = ref.shape[-1]
            for q in range(n):
                start = pl.multiple_of(off_ref[sem], 128)
                src = ref.at[q] if len(ref.shape) == 3 else ref
                mine.append(pltpu.make_async_copy(src, w_buf.at[s, :, pl.ds(start, cols)], w_sem.at[sem]))
                mine[-1].start()
                sem += 1
        at += len(pieces)
        waits.append(mine)
        if s == 0:
            t_waits = load_tokens()
    for cp in t_waits:
        cp.wait()
    ones = block_ones(t_buf.shape[0] // file_len, file_len, BF)
    for s, (_, first) in enumerate(plan):
        for cp in waits[s]:
            cp.wait()
        both = lax.dot_general(w_buf[s], t_buf[...], NT, preferred_element_type=F32)
        gate = both[:hid]
        units = (0.5 * gate * (1.0 + jnp.tanh(0.5 * gate)) * both[hid:]).astype(BF)
        new = lax.dot_general(ones, units, NT, preferred_element_type=F32)
        if first:
            outs[s][:first // file_len, :] = olds.pop(0)[...]
        outs[s][first // file_len:, :] = new


def ffn(toks, slices, firsts, offs, file_len, name, olds=()):
    width = toks[0].shape[1]
    n_rows = sum(t.shape[0] for t in toks)
    rows = slices[0][0].shape[-2]
    plan = tuple((tuple(p.shape[0] if p.ndim == 3 else 1 for p in s), f) for s, f in zip(slices, firsts))
    flat = [p for s in slices for p in s]
    vm, hbm = pl.BlockSpec(memory_space=pltpu.VMEM), pl.BlockSpec(memory_space=pl.ANY)
    return pl.pallas_call(
        functools.partial(ffn_kernel, plan, len(toks), file_len),
        in_specs=[pl.BlockSpec(memory_space=pltpu.SMEM)] + [hbm] * (len(toks) + len(flat)) + [vm] * len(olds),
        out_specs=tuple(vm for _ in slices),
        out_shape=tuple(jax.ShapeDtypeStruct(((n_rows + f) // file_len, rows // 2), F32) for f in firsts),
        scratch_shapes=[
            pltpu.VMEM((n_rows, width), BF),
            pltpu.VMEM((len(slices), rows, width), BF),
            pltpu.SemaphoreType.DMA((len(toks),)),
            pltpu.SemaphoreType.DMA((sum(sum(p) for p, _ in plan),)),
        ],
        compiler_params=pltpu.CompilerParams(vmem_limit_bytes=(16 + 4 * len(slices)) * 1024 * 1024),
        name=name,
    )(offs, *toks, *flat, *olds)


def down_kernel(files, pos_ref, u0, u1, u2, u3, w_ref, o_ref, buf):
    for k, u in enumerate((u0, u1, u2, u3)):
        for j in range(NX):
            dst = pl.multiple_of(pos_ref[k * NX + j], files)
            buf[pl.ds(dst, files), :] = u[j * files:(j + 1) * files, :]
    rows = buf[...]
    hi = rows.astype(BF)
    lo = (rows - hi.astype(F32)).astype(BF)
    w = w_ref[...]
    term = jnp.dot(hi, w, preferred_element_type=F32) + jnp.dot(lo, w, preferred_element_type=F32)
    o_ref[...] = term.astype(BF).reshape(o_ref.shape)


def down(us, w_down, pos, files):
    rows = NX * NY * files
    vm = pl.BlockSpec(memory_space=pltpu.VMEM)
    return pl.pallas_call(
        functools.partial(down_kernel, files),
        in_specs=[pl.BlockSpec(memory_space=pltpu.SMEM)] + [vm] * 5,
        out_specs=vm,
        out_shape=jax.ShapeDtypeStruct((NX * NY, files, w_down.shape[1]), BF),
        scratch_shapes=[pltpu.VMEM((rows, us[0].shape[1]), F32)],
        compiler_params=pltpu.CompilerParams(vmem_limit_bytes=16 * 1024 * 1024),
        name="down",
    )(pos, *us, w_down)


def emb_kernel(copies, t_ref, p_ref, len_ref, sel_ref, meta_ref, o_ref):
    total = p_ref[...]
    for m in range(t_ref.shape[0]):
        total = total + t_ref[m].astype(F32)
    pooled = total / len_ref[...]
    norm = lax.rsqrt(jnp.sum(pooled * pooled, axis=-1, keepdims=True) + 1e-06)
    emb = (pooled * norm).astype(BF)
    width = emb.shape[1]
    rows = jnp.dot(sel_ref[...], emb, preferred_element_type=F32)
    for d in range(sel_ref.shape[0] // 2):
        pair = rows[2 * d:2 * d + 2, :].astype(BF)
        about = meta_ref[2 * d:2 * d + 2, :].astype(BF)
        for m in range(copies):
            o_ref[d * copies + m, :, :width] = pair
            o_ref[d * copies + m, :, width:] = about


def emb_to_owners(terms, pooled, lens, sel, meta, copies):
    return pl.pallas_call(
        functools.partial(emb_kernel, copies),
        out_shape=jax.ShapeDtypeStruct((sel.shape[0] // 2 * copies, 2, pooled.shape[1] + meta.shape[1]), BF),
        compiler_params=pltpu.CompilerParams(vmem_limit_bytes=16 * 1024 * 1024),
        name="emb",
    )(terms, pooled, lens, sel, meta)


def match_kernel(mp_ref, rows_ref, bank_ref, key_ref, best_ref, sums_ref, about_ref, buf, sem):
    width = bank_ref.shape[1]
    n_blocks = sem.shape[0]
    block = bank_ref.shape[0] // n_blocks
    copies = []
    for i in range(n_blocks):
        at = pl.ds(i * block, block)
        copies.append(pltpu.make_async_copy(bank_ref.at[at], buf.at[at], sem.at[i]))
        copies[-1].start()
    rows, about = rows_ref[:, :width], rows_ref[:, width:]
    n = rows.shape[0]
    pick = lax.broadcasted_iota(I32, (8, 128), 0) == lax.broadcasted_iota(I32, (8, 128), 1)
    digits = lax.dot_general(jnp.where(pick, 1.0, 0.0).astype(BF), about, NT, preferred_element_type=F32)
    low = digits[0:1] * 65536.0 + digits[1:2] * 256.0 + digits[2:3]
    high = digits[3:4] * 65536.0 + digits[4:5] * 256.0 + digits[5:6]
    mine = digits[6:7] == (mp_ref[0] + 1).astype(F32)
    member = jnp.broadcast_to(jnp.where(mine, 1.0, 0.0), (8, n)).astype(BF)
    sums_ref[...] = jnp.dot(member, rows, preferred_element_type=F32)
    count = jnp.sum(jnp.where(mine, 1.0, 0.0), axis=1, keepdims=True)
    most = jnp.max(digits[7:8], axis=1, keepdims=True)
    about_ref[...] = jnp.where(lax.broadcasted_iota(I32, (1, 128), 1) == 0, count, most)
    for cp in copies:
        cp.wait()
    sims = lax.dot_general(buf[...], rows, NT, preferred_element_type=F32)
    key = key_ref[...]
    best = jnp.max(jnp.where((key >= low) & (key < high), sims, -1.0), axis=0, keepdims=True)
    n //= 2
    row, lane = (lax.broadcasted_iota(I32, (n, 2 * n), d) for d in (0, 1))
    best = jnp.broadcast_to(best, (n, 2 * n))
    pair = [jnp.max(jnp.where(lane == 2 * row + i, best, -1.0), axis=1, keepdims=True) for i in (0, 1)]
    out_lane = lax.broadcasted_iota(I32, (n, 128), 1)
    best_ref[:, 0, :] = jnp.where(out_lane == 0, pair[0], pair[1])


def match(rows, mp, bank, key):
    vm = pl.BlockSpec(memory_space=pltpu.VMEM)
    return pl.pallas_call(
        match_kernel,
        in_specs=[pl.BlockSpec(memory_space=pltpu.SMEM), vm, pl.BlockSpec(memory_space=pl.ANY), vm],
        out_specs=(vm, vm, vm),
        out_shape=(
            jax.ShapeDtypeStruct((rows.shape[0] // 2, 1, 128), F32),
            jax.ShapeDtypeStruct((8, bank.shape[1]), F32),
            jax.ShapeDtypeStruct((1, 128), F32),
        ),
        scratch_shapes=[pltpu.VMEM(bank.shape, BF), pltpu.SemaphoreType.DMA((8,))],
        compiler_params=pltpu.CompilerParams(vmem_limit_bytes=24 * 1024 * 1024),
        name="match",
    )(mp[None], rows, bank, key)


def on_device(
    hidden_in,
    mlp_gain,
    w_gate,
    w_up,
    w_down,
    lengths,
    file_cluster,
    file_order,
    cluster_slot,
    bank,
    bank_slot,
    bank_order,
    centroid_old,
    count_old,
):
    tok, width = hidden_in.shape
    files = lengths.shape[0]
    file_len = tok // files
    n_dp, n_mp = NZ * NC, NX * NY
    dp, mp = lax.axis_index("dp"), lax.axis_index("mp")
    z, c, x, y = dp // NC, dp % NC, mp // NY, mp % NY
    tie = lax.optimization_barrier

    k_total = cluster_slot.shape[0]
    owned = k_total // n_dp
    lookup = file_cluster[:, None] == jnp.arange(k_total, dtype=I32)[None, :]
    slot = jnp.sum(jnp.where(lookup, cluster_slot[None, :], 0), axis=1)
    owner = slot // owned
    ids = jnp.arange(files, dtype=I32)
    rank = jnp.sum(((owner[:, None] == owner[None, :]) & (ids[None, :] < ids[:, None])).astype(I32), axis=1)
    place = (owner[None, None, :] == jnp.arange(n_dp, dtype=I32)[:, None, None]) & (
        rank[None, None, :] == ids[None, :, None]
    )
    local = slot % owned
    first = local * ORDERS
    key = first + file_order
    bank_key = (bank_slot * ORDERS + bank_order).astype(F32)[:, None]
    low_key, high_key = [first >> 16, first * 0, first * 0], [key >> 16, (key >> 8) & 255, key & 255]
    digits = jnp.stack(low_key + high_key + [local + 1, jnp.broadcast_to(jnp.max(rank) + 1, slot.shape)], axis=1)

    def files_of(r):
        here = lax.dynamic_slice_in_dim(place, 2 * r, 2, 1)
        sel = here.reshape(-1, files)
        meta = jnp.sum(jnp.where(sel[:, :, None], digits[None], 0), axis=1).astype(F32)
        return here, sel.astype(BF), jnp.pad(meta, ((0, 0), (0, 120)))

    half, quarter = width // 2, width // 4
    w_t = [w_gate.T, w_up.T]
    w_h = jnp.concatenate([lax.dynamic_slice_in_dim(w, c * half, half, 1) for w in w_t], axis=0)
    normed, pooled_in = prep(hidden_in, mlp_gain, lengths)
    w_h, normed, w_t = tie((w_h, normed, w_t))
    t1, t2, t3 = from_x(normed, 1), from_x(normed, 2), from_x(normed, 3)
    h1, h3 = from_y(w_h, 1), from_y(w_h, 3)
    w_own = jnp.concatenate(w_t, axis=0)
    toks = [normed, t1, t2, t3]

    h_off = jnp.stack([c * half, (1 - c) * half]).astype(I32)
    e_off = jnp.stack([k * half + q * quarter for k in (c, 1 - c) for q in (0, 1)]).astype(I32)
    pos = jnp.stack(
        [(((x + j) % NX) * NY + (y - k) % NY) * files for k in range(NY) for j in range(NX)]
    ).astype(I32)
    lens = lengths.astype(F32)[:, None]
    ready = files_of(0)
    offs = jnp.concatenate([jnp.zeros((1,), I32), h_off, h_off])
    h1, h3, t2, pos, lens, ready = tie((h1, h3, t2, pos, lens, ready))
    toks = [normed, t1, t2, t3]
    s1, s3 = h1[:, :quarter], h3[:, quarter:]
    k2a, k2b = from_y(s1, 1), from_y(s3, 3)
    h1, h3 = tie((h1, h3, s1, s3, t1, t3))[:2]
    near = [[h1, from_core(h1)], [h3, from_core(h3)]]
    u0, u1, u3 = ffn(toks, [[w_own]] + near, (0,) * 3, offs, file_len, "ffn_main")
    r1, r3 = from_y(u1, NY - 1), from_y(u3, NY - 3)
    k2a, k2b, u0 = tie((k2a, k2b, u0))
    far = [k2a, k2b, from_core(k2a), from_core(k2b)]
    (u2,) = ffn(toks, [far], (0,), e_off, file_len, "ffn_far")
    r2 = from_y(u2, NY - 2)
    terms = down([u0, r1, r2, r3], w_down, pos, files)
    terms = lax.all_to_all(terms, "mp", 0, 0, tiled=True)

    def one_round(ready, best, sums, counts):
        here, sel, meta = ready
        rows = emb_to_owners(terms, pooled_in, lens, sel, meta, n_mp)
        rows = lax.all_to_all(rows, ALL, 0, 0, tiled=True)
        top, new, about = match(rows.reshape(-1, rows.shape[2]), mp, bank, bank_key)
        back = lax.all_to_all(top, ALL, 0, 0, tiled=True)
        back = jnp.max(back.reshape(n_dp, n_mp, -1), axis=1)[:, :2]
        best = jnp.maximum(best, jnp.max(jnp.where(here, back[:, :, None], -1.0), axis=(0, 1)))
        return about[0, 1], (best, sums + new[:1], counts + about[0, 0])

    most, state = one_round(ready, jnp.full((files,), -1.0, F32), jnp.zeros((1, width), F32), jnp.float32(0))
    _, (best, sums, counts) = lax.while_loop(
        lambda s: 2 * s[0] < most.astype(I32),
        lambda s: (s[0] + 1, one_round(files_of(s[0]), *s[1])[1]),
        (jnp.int32(1), state),
    )
    centroid_new = (count_old[:, None] * centroid_old + sums) / (count_old + counts)[:, None]
    return best, centroid_new


def solution(mesh):
    both = P(ALL)
    rows = P(ALL, None)
    return jax.shard_map(
        on_device,
        mesh=mesh,
        in_specs=(
            rows, P(), P(None, "mp"), P(None, "mp"), P("mp", None), both, both, both, P(), rows, both, both, rows, both,
        ),
        out_specs=(both, rows),
        check_vma=False,
    )
```

```python
import functools

import jax
import jax.numpy as jnp
from jax import lax
from jax.experimental import pallas as pl
from jax.experimental.pallas import tpu as pltpu
from jax.sharding import PartitionSpec as P

ALL = ("dp", "mp")
NX, NY, NZ, NC = 4, 4, 4, 2
ORDERS = 1 << 20
BF, F32, I32 = jnp.bfloat16, jnp.float32, jnp.int32
NT = (((1,), (1,)), ((), ()))


def from_x(v, j):
    perm = [(((x + j) % NX) * NY + y, x * NY + y) for x in range(NX) for y in range(NY)]
    return lax.ppermute(v, "mp", perm)


def from_y(v, k):
    perm = [(x * NY + (y + k) % NY, x * NY + y) for x in range(NX) for y in range(NY)]
    return lax.ppermute(v, "mp", perm)


def from_core(v):
    return lax.ppermute(v, "dp", [(d ^ 1, d) for d in range(NZ * NC)])


def block_ones(files, file_len, dtype):
    row = lax.broadcasted_iota(I32, (files, files * file_len), 0)
    col = lax.broadcasted_iota(I32, (files, files * file_len), 1)
    return jnp.where(col // file_len == row, 1.0, 0.0).astype(dtype)


def prep_kernel(file_len, len_ref, h_ref, gain_ref, n_ref, p_ref):
    gain = gain_ref[...].astype(F32)
    ones = jnp.ones((p_ref.shape[0], file_len), BF)
    for f in range(p_ref.shape[0]):
        rows = slice(f * file_len, (f + 1) * file_len)
        raw = h_ref[rows, :]
        resid = raw.astype(F32)
        scale = lax.rsqrt(jnp.mean(resid * resid, axis=-1, keepdims=True) + 1e-05)
        keep = lax.broadcasted_iota(I32, (file_len, 1), 0) < len_ref[f]
        n_ref[rows, :] = jnp.where(keep, resid * scale * gain, 0.0).astype(BF)
        valid = jnp.where(keep, resid, 0.0).astype(BF)
        p_ref[f:f + 1, :] = jnp.dot(ones, valid, preferred_element_type=F32)[:1]


def prep(hidden, gain, lengths):
    tok, width = hidden.shape
    files = lengths.shape[0]
    vm = pl.BlockSpec(memory_space=pltpu.VMEM)
    return pl.pallas_call(
        functools.partial(prep_kernel, tok // files),
        in_specs=[pl.BlockSpec(memory_space=pltpu.SMEM), vm, vm],
        out_specs=(vm, vm),
        out_shape=(jax.ShapeDtypeStruct((tok, width), BF), jax.ShapeDtypeStruct((files, width), F32)),
        compiler_params=pltpu.CompilerParams(vmem_limit_bytes=16 * 1024 * 1024),
        name="prep",
    )(lengths, hidden, gain[None, :])


def ffn_kernel(plan, n_tok, file_len, off_ref, *refs):
    n_parts = sum(len(p) for p, _ in plan)
    n_old = sum(1 for _, first in plan if first)
    toks, refs = refs[:n_tok], refs[n_tok:]
    parts, refs = refs[:n_parts], refs[n_parts:]
    olds, refs = list(refs[:n_old]), refs[n_old:]
    outs, refs = refs[:len(plan)], refs[len(plan):]
    t_buf, w_buf, t_sem, w_sem = refs
    hid = w_buf.shape[1] // 2

    def load_tokens():
        row, done = 0, []
        for t in range(n_tok):
            rows = toks[t].shape[0]
            done.append(pltpu.make_async_copy(toks[t], t_buf.at[pl.ds(row, rows)], t_sem.at[t]))
            done[-1].start()
            row += rows
        return done

    at, sem, waits = 0, 0, []
    for s, (pieces, _) in enumerate(plan):
        mine = []
        for p, n in enumerate(pieces):
            ref = parts[at + p]
            cols = ref.shape[-1]
            for q in range(n):
                start = pl.multiple_of(off_ref[sem], 128)
                src = ref.at[q] if len(ref.shape) == 3 else ref
                mine.append(pltpu.make_async_copy(src, w_buf.at[s, :, pl.ds(start, cols)], w_sem.at[sem]))
                mine[-1].start()
                sem += 1
        at += len(pieces)
        waits.append(mine)
        if s == 0:
            t_waits = load_tokens()
    for cp in t_waits:
        cp.wait()
    ones = block_ones(t_buf.shape[0] // file_len, file_len, BF)
    for s, (_, first) in enumerate(plan):
        for cp in waits[s]:
            cp.wait()
        both = lax.dot_general(w_buf[s], t_buf[...], NT, preferred_element_type=F32)
        gate = both[:hid]
        units = (0.5 * gate * (1.0 + jnp.tanh(0.5 * gate)) * both[hid:]).astype(BF)
        new = lax.dot_general(ones, units, NT, preferred_element_type=F32)
        if first:
            outs[s][:first // file_len, :] = olds.pop(0)[...]
        outs[s][first // file_len:, :] = new


def ffn(toks, slices, firsts, offs, file_len, name, olds=()):
    width = toks[0].shape[1]
    n_rows = sum(t.shape[0] for t in toks)
    rows = slices[0][0].shape[-2]
    plan = tuple((tuple(p.shape[0] if p.ndim == 3 else 1 for p in s), f) for s, f in zip(slices, firsts))
    flat = [p for s in slices for p in s]
    vm, hbm = pl.BlockSpec(memory_space=pltpu.VMEM), pl.BlockSpec(memory_space=pl.ANY)
    return pl.pallas_call(
        functools.partial(ffn_kernel, plan, len(toks), file_len),
        in_specs=[pl.BlockSpec(memory_space=pltpu.SMEM)] + [hbm] * (len(toks) + len(flat)) + [vm] * len(olds),
        out_specs=tuple(vm for _ in slices),
        out_shape=tuple(jax.ShapeDtypeStruct(((n_rows + f) // file_len, rows // 2), F32) for f in firsts),
        scratch_shapes=[
            pltpu.VMEM((n_rows, width), BF),
            pltpu.VMEM((len(slices), rows, width), BF),
            pltpu.SemaphoreType.DMA((len(toks),)),
            pltpu.SemaphoreType.DMA((sum(sum(p) for p, _ in plan),)),
        ],
        compiler_params=pltpu.CompilerParams(vmem_limit_bytes=(16 + 4 * len(slices)) * 1024 * 1024),
        name=name,
    )(offs, *toks, *flat, *olds)


def down_kernel(files, pos_ref, u0, u1, u2, u3, w_ref, o_ref, buf):
    for k, u in enumerate((u0, u1, u2, u3)):
        for j in range(NX):
            dst = pl.multiple_of(pos_ref[k * NX + j], files)
            buf[pl.ds(dst, files), :] = u[j * files:(j + 1) * files, :]
    rows = buf[...]
    hi = rows.astype(BF)
    lo = (rows - hi.astype(F32)).astype(BF)
    w = w_ref[...]
    term = jnp.dot(hi, w, preferred_element_type=F32) + jnp.dot(lo, w, preferred_element_type=F32)
    o_ref[...] = term.astype(BF).reshape(o_ref.shape)


def down(us, w_down, pos, files):
    rows = NX * NY * files
    vm = pl.BlockSpec(memory_space=pltpu.VMEM)
    return pl.pallas_call(
        functools.partial(down_kernel, files),
        in_specs=[pl.BlockSpec(memory_space=pltpu.SMEM)] + [vm] * 5,
        out_specs=vm,
        out_shape=jax.ShapeDtypeStruct((NX * NY, files, w_down.shape[1]), BF),
        scratch_shapes=[pltpu.VMEM((rows, us[0].shape[1]), F32)],
        compiler_params=pltpu.CompilerParams(vmem_limit_bytes=16 * 1024 * 1024),
        name="down",
    )(pos, *us, w_down)


def emb_kernel(copies, t_ref, p_ref, len_ref, sel_ref, meta_ref, o_ref):
    total = p_ref[...]
    for m in range(t_ref.shape[0]):
        total = total + t_ref[m].astype(F32)
    pooled = total / len_ref[...]
    norm = lax.rsqrt(jnp.sum(pooled * pooled, axis=-1, keepdims=True) + 1e-06)
    emb = (pooled * norm).astype(BF)
    width = emb.shape[1]
    rows = jnp.dot(sel_ref[...], emb, preferred_element_type=F32)
    for d in range(sel_ref.shape[0] // 2):
        pair = rows[2 * d:2 * d + 2, :].astype(BF)
        about = meta_ref[2 * d:2 * d + 2, :].astype(BF)
        for m in range(copies):
            o_ref[d * copies + m, :, :width] = pair
            o_ref[d * copies + m, :, width:] = about


def emb_to_owners(terms, pooled, lens, sel, meta, copies):
    return pl.pallas_call(
        functools.partial(emb_kernel, copies),
        out_shape=jax.ShapeDtypeStruct((sel.shape[0] // 2 * copies, 2, pooled.shape[1] + meta.shape[1]), BF),
        compiler_params=pltpu.CompilerParams(vmem_limit_bytes=16 * 1024 * 1024),
        name="emb",
    )(terms, pooled, lens, sel, meta)


def match_kernel(mp_ref, rows_ref, bank_ref, key_ref, best_ref, sums_ref, about_ref, buf, sem):
    width = bank_ref.shape[1]
    n_blocks = sem.shape[0]
    block = bank_ref.shape[0] // n_blocks
    copies = []
    for i in range(n_blocks):
        at = pl.ds(i * block, block)
        copies.append(pltpu.make_async_copy(bank_ref.at[at], buf.at[at], sem.at[i]))
        copies[-1].start()
    rows, about = rows_ref[:, :width], rows_ref[:, width:]
    n = rows.shape[0]
    pick = lax.broadcasted_iota(I32, (8, 128), 0) == lax.broadcasted_iota(I32, (8, 128), 1)
    digits = lax.dot_general(jnp.where(pick, 1.0, 0.0).astype(BF), about, NT, preferred_element_type=F32)
    low = digits[0:1] * 65536.0 + digits[1:2] * 256.0 + digits[2:3]
    high = digits[3:4] * 65536.0 + digits[4:5] * 256.0 + digits[5:6]
    mine = digits[6:7] == (mp_ref[0] + 1).astype(F32)
    member = jnp.broadcast_to(jnp.where(mine, 1.0, 0.0), (8, n)).astype(BF)
    sums_ref[...] = jnp.dot(member, rows, preferred_element_type=F32)
    count = jnp.sum(jnp.where(mine, 1.0, 0.0), axis=1, keepdims=True)
    most = jnp.max(digits[7:8], axis=1, keepdims=True)
    about_ref[...] = jnp.where(lax.broadcasted_iota(I32, (1, 128), 1) == 0, count, most)
    for cp in copies:
        cp.wait()
    sims = lax.dot_general(buf[...], rows, NT, preferred_element_type=F32)
    key = key_ref[...]
    best = jnp.max(jnp.where((key >= low) & (key < high), sims, -1.0), axis=0, keepdims=True)
    n //= 2
    row, lane = (lax.broadcasted_iota(I32, (n, 2 * n), d) for d in (0, 1))
    best = jnp.broadcast_to(best, (n, 2 * n))
    pair = [jnp.max(jnp.where(lane == 2 * row + i, best, -1.0), axis=1, keepdims=True) for i in (0, 1)]
    out_lane = lax.broadcasted_iota(I32, (n, 128), 1)
    best_ref[:, 0, :] = jnp.where(out_lane == 0, pair[0], pair[1])


def match(rows, mp, bank, key):
    vm = pl.BlockSpec(memory_space=pltpu.VMEM)
    return pl.pallas_call(
        match_kernel,
        in_specs=[pl.BlockSpec(memory_space=pltpu.SMEM), vm, pl.BlockSpec(memory_space=pl.ANY), vm],
        out_specs=(vm, vm, vm),
        out_shape=(
            jax.ShapeDtypeStruct((rows.shape[0] // 2, 1, 128), F32),
            jax.ShapeDtypeStruct((8, bank.shape[1]), F32),
            jax.ShapeDtypeStruct((1, 128), F32),
        ),
        scratch_shapes=[pltpu.VMEM(bank.shape, BF), pltpu.SemaphoreType.DMA((8,))],
        compiler_params=pltpu.CompilerParams(vmem_limit_bytes=24 * 1024 * 1024),
        name="match",
    )(mp[None], rows, bank, key)


def on_device(
    hidden_in,
    mlp_gain,
    w_gate,
    w_up,
    w_down,
    lengths,
    file_cluster,
    file_order,
    cluster_slot,
    bank,
    bank_slot,
    bank_order,
    centroid_old,
    count_old,
):
    tok, width = hidden_in.shape
    files = lengths.shape[0]
    file_len = tok // files
    n_dp, n_mp = NZ * NC, NX * NY
    dp, mp = lax.axis_index("dp"), lax.axis_index("mp")
    z, c, x, y = dp // NC, dp % NC, mp // NY, mp % NY
    tie = lax.optimization_barrier

    k_total = cluster_slot.shape[0]
    owned = k_total // n_dp
    lookup = file_cluster[:, None] == jnp.arange(k_total, dtype=I32)[None, :]
    slot = jnp.sum(jnp.where(lookup, cluster_slot[None, :], 0), axis=1)
    owner = slot // owned
    ids = jnp.arange(files, dtype=I32)
    rank = jnp.sum(((owner[:, None] == owner[None, :]) & (ids[None, :] < ids[:, None])).astype(I32), axis=1)
    place = (owner[None, None, :] == jnp.arange(n_dp, dtype=I32)[:, None, None]) & (
        rank[None, None, :] == ids[None, :, None]
    )
    local = slot % owned
    first = local * ORDERS
    key = first + file_order
    bank_key = (bank_slot * ORDERS + bank_order).astype(F32)[:, None]
    low_key, high_key = [first >> 16, first * 0, first * 0], [key >> 16, (key >> 8) & 255, key & 255]
    digits = jnp.stack(low_key + high_key + [local + 1, jnp.broadcast_to(jnp.max(rank) + 1, slot.shape)], axis=1)

    def files_of(r):
        here = lax.dynamic_slice_in_dim(place, 2 * r, 2, 1)
        sel = here.reshape(-1, files)
        meta = jnp.sum(jnp.where(sel[:, :, None], digits[None], 0), axis=1).astype(F32)
        return here, sel.astype(BF), jnp.pad(meta, ((0, 0), (0, 120)))

    half, quarter = width // 2, width // 4
    w_t = [w_gate.T, w_up.T]
    w_h = jnp.concatenate([lax.dynamic_slice_in_dim(w, c * half, half, 1) for w in w_t], axis=0)
    w_h, hidden_in, w_t = tie((w_h, hidden_in, w_t))
    normed, pooled_in = prep(hidden_in, mlp_gain, lengths)
    t1, t3 = from_x(normed, 1), from_x(normed, 3)
    h1, h3 = from_y(w_h, 1), from_y(w_h, 3)
    w_own = jnp.concatenate(w_t, axis=0)
    t1, t3 = tie((t1, t3))
    t2a, t2b = from_x(t1[:tok // 2], 1), from_x(t3[tok // 2:], 3)
    toks, last = [normed, t1, t3], [t2a, t2b]

    h_off = jnp.stack([c * half, (1 - c) * half]).astype(I32)
    e_off = jnp.stack([k * half + q * quarter for k in (c, 1 - c) for q in (0, 1)]).astype(I32)
    pos = jnp.stack(
        [(((x + j) % NX) * NY + (y - k) % NY) * files for k in range(NY) for j in (0, 1, 3, 2)]
    ).astype(I32)
    lens = lengths.astype(F32)[:, None]
    ready = files_of(0)
    normed, e_off, h_off, pos, lens, bank_key, ready = tie((normed, e_off, h_off, pos, lens, bank_key, ready))
    toks[0] = normed

    zero = jnp.zeros((1,), I32)
    (u0,) = ffn(toks, [[w_own]], (0,), zero, file_len, "ffn_own")
    h1, h3, u0 = tie((h1, h3, u0))
    k2a, k2b = from_y(h1[:, :quarter], 1), from_y(h3[:, quarter:], 3)
    near = [[h1, from_core(h1)], [h3, from_core(h3)]]
    near_off = jnp.concatenate([h_off, h_off])
    u1, u3 = ffn(toks, near, (0, 0), near_off, file_len, "ffn_near")
    first = sum(t.shape[0] for t in toks)
    k2a, k2b, u1, u3, last = tie((k2a, k2b, u1, u3, last))
    far = [k2a, k2b, from_core(k2a), from_core(k2b)]
    rest = jnp.concatenate([near_off, zero])
    u1, u3, u0 = ffn(last, near + [[w_own]], (first,) * 3, rest, file_len, "ffn_rest", (u1, u3, u0))
    r1, r3 = from_y(u1, NY - 1), from_y(u3, NY - 3)
    (u2,) = ffn(toks + last, [far], (0,), e_off, file_len, "ffn_far")
    r2 = from_y(u2, NY - 2)
    terms = down([u0, r1, r2, r3], w_down, pos, files)
    terms = lax.all_to_all(terms, "mp", 0, 0, tiled=True)

    def one_round(ready, best, sums, counts):
        here, sel, meta = ready
        rows = emb_to_owners(terms, pooled_in, lens, sel, meta, n_mp)
        rows = lax.all_to_all(rows, ALL, 0, 0, tiled=True)
        top, new, about = match(rows.reshape(-1, rows.shape[2]), mp, bank, bank_key)
        back = lax.all_to_all(top, ALL, 0, 0, tiled=True)
        back = jnp.max(back.reshape(n_dp, n_mp, -1), axis=1)[:, :2]
        best = jnp.maximum(best, jnp.max(jnp.where(here, back[:, :, None], -1.0), axis=(0, 1)))
        return about[0, 1], (best, sums + new[:1], counts + about[0, 0])

    most, state = one_round(ready, jnp.full((files,), -1.0, F32), jnp.zeros((1, width), F32), jnp.float32(0))
    _, (best, sums, counts) = lax.while_loop(
        lambda s: 2 * s[0] < most.astype(I32),
        lambda s: (s[0] + 1, one_round(files_of(s[0]), *s[1])[1]),
        (jnp.int32(1), state),
    )
    centroid_new = (count_old[:, None] * centroid_old + sums) / (count_old + counts)[:, None]
    return best, centroid_new


def solution(mesh):
    both = P(ALL)
    rows = P(ALL, None)
    return jax.shard_map(
        on_device,
        mesh=mesh,
        in_specs=(
            rows, P(), P(None, "mp"), P(None, "mp"), P("mp", None), both, both, both, P(), rows, both, both, rows, both,
        ),
        out_specs=(both, rows),
        check_vma=False,
    )
```

```python
import functools

import jax
import jax.numpy as jnp
from jax import lax
from jax.experimental import pallas as pl
from jax.experimental.pallas import tpu as pltpu
from jax.sharding import PartitionSpec as P

ALL = ("dp", "mp")
NX, NY, NZ, NC = 4, 4, 4, 2
ORDERS = 1 << 20
BF, F32, I32 = jnp.bfloat16, jnp.float32, jnp.int32
NT = (((1,), (1,)), ((), ()))


def from_x(v, j):
    perm = [(((x + j) % NX) * NY + y, x * NY + y) for x in range(NX) for y in range(NY)]
    return lax.ppermute(v, "mp", perm)


def from_y(v, k):
    perm = [(x * NY + (y + k) % NY, x * NY + y) for x in range(NX) for y in range(NY)]
    return lax.ppermute(v, "mp", perm)


def from_core(v):
    return lax.ppermute(v, "dp", [(d ^ 1, d) for d in range(NZ * NC)])


def block_ones(files, file_len, dtype):
    row = lax.broadcasted_iota(I32, (files, files * file_len), 0)
    col = lax.broadcasted_iota(I32, (files, files * file_len), 1)
    return jnp.where(col // file_len == row, 1.0, 0.0).astype(dtype)


def prep_kernel(file_len, len_ref, h_ref, gain_ref, n_ref, p_ref):
    gain = gain_ref[...].astype(F32)
    ones = jnp.ones((p_ref.shape[0], file_len), BF)
    for f in range(p_ref.shape[0]):
        rows = slice(f * file_len, (f + 1) * file_len)
        raw = h_ref[rows, :]
        resid = raw.astype(F32)
        scale = lax.rsqrt(jnp.mean(resid * resid, axis=-1, keepdims=True) + 1e-05)
        keep = lax.broadcasted_iota(I32, (file_len, 1), 0) < len_ref[f]
        n_ref[rows, :] = jnp.where(keep, resid * scale * gain, 0.0).astype(BF)
        valid = jnp.where(keep, resid, 0.0).astype(BF)
        p_ref[f:f + 1, :] = jnp.dot(ones, valid, preferred_element_type=F32)[:1]


def prep(hidden, gain, lengths):
    tok, width = hidden.shape
    files = lengths.shape[0]
    vm = pl.BlockSpec(memory_space=pltpu.VMEM)
    return pl.pallas_call(
        functools.partial(prep_kernel, tok // files),
        in_specs=[pl.BlockSpec(memory_space=pltpu.SMEM), vm, vm],
        out_specs=(vm, vm),
        out_shape=(jax.ShapeDtypeStruct((tok, width), BF), jax.ShapeDtypeStruct((files, width), F32)),
        compiler_params=pltpu.CompilerParams(vmem_limit_bytes=16 * 1024 * 1024),
        name="prep",
    )(lengths, hidden, gain[None, :])


def cut_kernel(a_ref, b_ref, left_ref, right_ref, sem):
    cols = left_ref.shape[1]
    copies = [
        pltpu.make_async_copy(a_ref.at[:, pl.ds(0, cols)], left_ref, sem.at[0]),
        pltpu.make_async_copy(b_ref.at[:, pl.ds(cols, cols)], right_ref, sem.at[1]),
    ]
    for cp in copies:
        cp.start()
    for cp in copies:
        cp.wait()


def cut_halves(a, b):
    hbm = pl.BlockSpec(memory_space=pl.ANY)
    out = jax.ShapeDtypeStruct((a.shape[0], a.shape[1] // 2), a.dtype)
    return pl.pallas_call(
        cut_kernel,
        in_specs=[hbm, hbm],
        out_specs=(hbm, hbm),
        out_shape=(out, out),
        scratch_shapes=[pltpu.SemaphoreType.DMA((2,))],
        name="cut",
    )(a, b)


def ffn_kernel(plan, n_tok, file_len, off_ref, *refs):
    n_parts = sum(len(p) for p, _ in plan)
    n_old = sum(1 for _, first in plan if first)
    toks, refs = refs[:n_tok], refs[n_tok:]
    parts, refs = refs[:n_parts], refs[n_parts:]
    olds, refs = list(refs[:n_old]), refs[n_old:]
    outs, refs = refs[:len(plan)], refs[len(plan):]
    t_buf, w_buf, t_sem, w_sem = refs
    hid = w_buf.shape[1] // 2

    def load_tokens():
        row, done = 0, []
        for t in range(n_tok):
            rows = toks[t].shape[0]
            done.append(pltpu.make_async_copy(toks[t], t_buf.at[pl.ds(row, rows)], t_sem.at[t]))
            done[-1].start()
            row += rows
        return done

    at, sem, waits = 0, 0, []
    for s, (pieces, _) in enumerate(plan):
        mine = []
        for p, n in enumerate(pieces):
            ref = parts[at + p]
            cols = ref.shape[-1]
            for q in range(n):
                start = pl.multiple_of(off_ref[sem], 128)
                src = ref.at[q] if len(ref.shape) == 3 else ref
                mine.append(pltpu.make_async_copy(src, w_buf.at[s, :, pl.ds(start, cols)], w_sem.at[sem]))
                mine[-1].start()
                sem += 1
        at += len(pieces)
        waits.append(mine)
        if s == 0:
            t_waits = load_tokens()
    for cp in t_waits:
        cp.wait()
    ones = block_ones(t_buf.shape[0] // file_len, file_len, BF)
    for s, (_, first) in enumerate(plan):
        for cp in waits[s]:
            cp.wait()
        both = lax.dot_general(w_buf[s], t_buf[...], NT, preferred_element_type=F32)
        gate = both[:hid]
        units = (0.5 * gate * (1.0 + jnp.tanh(0.5 * gate)) * both[hid:]).astype(BF)
        new = lax.dot_general(ones, units, NT, preferred_element_type=F32)
        if first:
            outs[s][:first // file_len, :] = olds.pop(0)[...]
        outs[s][first // file_len:, :] = new


def ffn(toks, slices, firsts, offs, file_len, name, olds=()):
    width = toks[0].shape[1]
    n_rows = sum(t.shape[0] for t in toks)
    rows = slices[0][0].shape[-2]
    plan = tuple((tuple(p.shape[0] if p.ndim == 3 else 1 for p in s), f) for s, f in zip(slices, firsts))
    flat = [p for s in slices for p in s]
    vm, hbm = pl.BlockSpec(memory_space=pltpu.VMEM), pl.BlockSpec(memory_space=pl.ANY)
    return pl.pallas_call(
        functools.partial(ffn_kernel, plan, len(toks), file_len),
        in_specs=[pl.BlockSpec(memory_space=pltpu.SMEM)] + [hbm] * (len(toks) + len(flat)) + [vm] * len(olds),
        out_specs=tuple(vm for _ in slices),
        out_shape=tuple(jax.ShapeDtypeStruct(((n_rows + f) // file_len, rows // 2), F32) for f in firsts),
        scratch_shapes=[
            pltpu.VMEM((n_rows, width), BF),
            pltpu.VMEM((len(slices), rows, width), BF),
            pltpu.SemaphoreType.DMA((len(toks),)),
            pltpu.SemaphoreType.DMA((sum(sum(p) for p, _ in plan),)),
        ],
        compiler_params=pltpu.CompilerParams(vmem_limit_bytes=(16 + 4 * len(slices)) * 1024 * 1024),
        name=name,
    )(offs, *toks, *flat, *olds)


def down_kernel(files, pos_ref, u0, u1, u2, u3, w_ref, o_ref, buf):
    for k, u in enumerate((u0, u1, u2, u3)):
        for j in range(NX):
            dst = pl.multiple_of(pos_ref[k * NX + j], files)
            buf[pl.ds(dst, files), :] = u[j * files:(j + 1) * files, :]
    rows = buf[...]
    hi = rows.astype(BF)
    lo = (rows - hi.astype(F32)).astype(BF)
    w = w_ref[...]
    term = jnp.dot(hi, w, preferred_element_type=F32) + jnp.dot(lo, w, preferred_element_type=F32)
    o_ref[...] = term.astype(BF).reshape(o_ref.shape)


def down(us, w_down, pos, files):
    rows = NX * NY * files
    vm = pl.BlockSpec(memory_space=pltpu.VMEM)
    return pl.pallas_call(
        functools.partial(down_kernel, files),
        in_specs=[pl.BlockSpec(memory_space=pltpu.SMEM)] + [vm] * 5,
        out_specs=vm,
        out_shape=jax.ShapeDtypeStruct((NX * NY, files, w_down.shape[1]), BF),
        scratch_shapes=[pltpu.VMEM((rows, us[0].shape[1]), F32)],
        compiler_params=pltpu.CompilerParams(vmem_limit_bytes=16 * 1024 * 1024),
        name="down",
    )(pos, *us, w_down)


def emb_kernel(copies, t_ref, p_ref, len_ref, sel_ref, meta_ref, o_ref):
    total = p_ref[...]
    for m in range(t_ref.shape[0]):
        total = total + t_ref[m].astype(F32)
    pooled = total / len_ref[...]
    norm = lax.rsqrt(jnp.sum(pooled * pooled, axis=-1, keepdims=True) + 1e-06)
    emb = (pooled * norm).astype(BF)
    width = emb.shape[1]
    rows = jnp.dot(sel_ref[...], emb, preferred_element_type=F32)
    for d in range(sel_ref.shape[0] // 2):
        pair = rows[2 * d:2 * d + 2, :].astype(BF)
        about = meta_ref[2 * d:2 * d + 2, :].astype(BF)
        for m in range(copies):
            o_ref[d * copies + m, :, :width] = pair
            o_ref[d * copies + m, :, width:] = about


def emb_to_owners(terms, pooled, lens, sel, meta, copies):
    return pl.pallas_call(
        functools.partial(emb_kernel, copies),
        out_shape=jax.ShapeDtypeStruct((sel.shape[0] // 2 * copies, 2, pooled.shape[1] + meta.shape[1]), BF),
        compiler_params=pltpu.CompilerParams(vmem_limit_bytes=16 * 1024 * 1024),
        name="emb",
    )(terms, pooled, lens, sel, meta)


def match_kernel(mp_ref, rows_ref, bank_ref, key_ref, best_ref, sums_ref, about_ref, buf, sem):
    width = bank_ref.shape[1]
    n_blocks = sem.shape[0]
    block = bank_ref.shape[0] // n_blocks
    copies = []
    for i in range(n_blocks):
        at = pl.ds(i * block, block)
        copies.append(pltpu.make_async_copy(bank_ref.at[at], buf.at[at], sem.at[i]))
        copies[-1].start()
    rows = rows_ref[:, :width]
    n = rows.shape[0]
    digits = rows_ref[:, width:].astype(F32)
    low = digits[:, 0:1] * 65536.0 + digits[:, 1:2] * 256.0 + digits[:, 2:3]
    high = digits[:, 3:4] * 65536.0 + digits[:, 4:5] * 256.0 + digits[:, 5:6]
    mine = jnp.where(digits[:, 6:7] == (mp_ref[0] + 1).astype(F32), 1.0, 0.0)
    member = jnp.broadcast_to(mine, (n, 8)).astype(BF)
    sums_ref[...] = lax.dot_general(member, rows, (((0,), (0,)), ((), ())), preferred_element_type=F32)
    count = jnp.sum(mine, axis=0, keepdims=True)
    most = jnp.max(digits[:, 7:8], axis=0, keepdims=True)
    about_ref[...] = jnp.where(lax.broadcasted_iota(I32, (1, 128), 1) == 0, count, most)
    best = jnp.full((n, 1), -1.0, F32)
    block *= n_blocks // 2
    for i in range(2):
        for cp in copies[i * n_blocks // 2:(i + 1) * n_blocks // 2]:
            cp.wait()
        at = slice(i * block, (i + 1) * block)
        sims = lax.dot_general(rows, buf[at, :], NT, preferred_element_type=F32)
        key = key_ref[:, at]
        best = jnp.maximum(best, jnp.max(jnp.where((key >= low) & (key < high), sims, -1.0), axis=1, keepdims=True))
    best_ref[:, 0, :] = jnp.broadcast_to(best, (n, 128))


def match(rows, mp, bank, key):
    vm = pl.BlockSpec(memory_space=pltpu.VMEM)
    return pl.pallas_call(
        match_kernel,
        in_specs=[pl.BlockSpec(memory_space=pltpu.SMEM), vm, pl.BlockSpec(memory_space=pl.ANY), vm],
        out_specs=(vm, vm, vm),
        out_shape=(
            jax.ShapeDtypeStruct((rows.shape[0], 1, 128), F32),
            jax.ShapeDtypeStruct((8, bank.shape[1]), F32),
            jax.ShapeDtypeStruct((1, 128), F32),
        ),
        scratch_shapes=[pltpu.VMEM(bank.shape, BF), pltpu.SemaphoreType.DMA((8,))],
        compiler_params=pltpu.CompilerParams(vmem_limit_bytes=24 * 1024 * 1024),
        name="match",
    )(mp[None], rows, bank, key)


def on_device(
    hidden_in,
    mlp_gain,
    w_gate,
    w_up,
    w_down,
    lengths,
    file_cluster,
    file_order,
    cluster_slot,
    bank,
    bank_slot,
    bank_order,
    centroid_old,
    count_old,
):
    tok, width = hidden_in.shape
    files = lengths.shape[0]
    file_len = tok // files
    n_dp, n_mp = NZ * NC, NX * NY
    dp, mp = lax.axis_index("dp"), lax.axis_index("mp")
    z, c, x, y = dp // NC, dp % NC, mp // NY, mp % NY
    tie = lax.optimization_barrier

    k_total = cluster_slot.shape[0]
    owned = k_total // n_dp
    lookup = file_cluster[:, None] == jnp.arange(k_total, dtype=I32)[None, :]
    slot = jnp.sum(jnp.where(lookup, cluster_slot[None, :], 0), axis=1)
    owner = slot // owned
    ids = jnp.arange(files, dtype=I32)
    rank = jnp.sum(((owner[:, None] == owner[None, :]) & (ids[None, :] < ids[:, None])).astype(I32), axis=1)
    place = (owner[None, None, :] == jnp.arange(n_dp, dtype=I32)[:, None, None]) & (
        rank[None, None, :] == ids[None, :, None]
    )
    local = slot % owned
    first = local * ORDERS
    key = first + file_order
    bank_key = (bank_slot * ORDERS + bank_order).astype(F32)[None, :]
    low_key, high_key = [first >> 16, first * 0, first * 0], [key >> 16, (key >> 8) & 255, key & 255]
    digits = jnp.stack(low_key + high_key + [local + 1, jnp.broadcast_to(jnp.max(rank) + 1, slot.shape)], axis=1)

    def files_of(r):
        here = lax.dynamic_slice_in_dim(place, 2 * r, 2, 1)
        sel = here.reshape(-1, files)
        meta = jnp.sum(jnp.where(sel[:, :, None], digits[None], 0), axis=1).astype(F32)
        return here, sel.astype(BF), jnp.pad(meta, ((0, 0), (0, 120)))

    half, quarter = width // 2, width // 4
    w_t = [w_gate.T, w_up.T]
    w_h = jnp.concatenate([lax.dynamic_slice_in_dim(w, c * half, half, 1) for w in w_t], axis=0)
    w_h, hidden_in, w_t = tie((w_h, hidden_in, w_t))
    normed, pooled_in = prep(hidden_in, mlp_gain, lengths)
    t1, t3 = from_x(normed, 1), from_x(normed, 3)
    h1, h3 = from_y(w_h, 1), from_y(w_h, 3)
    w_own = jnp.concatenate(w_t, axis=0)
    t1, t3 = tie((t1, t3))
    t2a, t2b = from_x(t1[:tok // 2], 1), from_x(t3[tok // 2:], 3)
    toks, last = [normed, t1, t3], [t2a, t2b]

    h_off = jnp.stack([c * half, (1 - c) * half]).astype(I32)
    e_off = jnp.stack([k * half + q * quarter for k in (c, 1 - c) for q in (0, 1)]).astype(I32)
    pos = jnp.stack(
        [(((x + j) % NX) * NY + (y - k) % NY) * files for k in range(NY) for j in (0, 1, 3, 2)]
    ).astype(I32)
    lens = lengths.astype(F32)[:, None]
    ready = files_of(0)
    normed, e_off, h_off, pos, lens, bank_key, ready = tie((normed, e_off, h_off, pos, lens, bank_key, ready))
    toks[0] = normed

    zero = jnp.zeros((1,), I32)
    (u0,) = ffn(toks, [[w_own]], (0,), zero, file_len, "ffn_own")
    h1, h3, u0 = tie((h1, h3, u0))
    left, right = cut_halves(h1, h3)
    k2a, k2b = from_y(left, 1), from_y(right, 3)
    near = [[h1, from_core(h1)], [h3, from_core(h3)]]
    near_off = jnp.concatenate([h_off, h_off])
    u1, u3 = ffn(toks, near, (0, 0), near_off, file_len, "ffn_near")
    first = sum(t.shape[0] for t in toks)
    k2a, k2b, u1, u3, last = tie((k2a, k2b, u1, u3, last))
    far = [k2a, k2b, from_core(k2a), from_core(k2b)]
    rest = jnp.concatenate([near_off, zero])
    u1, u3, u0 = ffn(last, near + [[w_own]], (first,) * 3, rest, file_len, "ffn_rest", (u1, u3, u0))
    r1, r3 = from_y(u1, NY - 1), from_y(u3, NY - 3)
    (u2,) = ffn(toks + last, [far], (0,), e_off, file_len, "ffn_far")
    r2 = from_y(u2, NY - 2)
    terms = down([u0, r1, r2, r3], w_down, pos, files)
    terms = lax.all_to_all(terms, "mp", 0, 0, tiled=True)

    def one_round(ready, best, sums, counts, _):
        here, sel, meta = ready
        rows = emb_to_owners(terms, pooled_in, lens, sel, meta, n_mp)
        rows = lax.all_to_all(rows, ALL, 0, 0, tiled=True)
        top, new, about = match(rows.reshape(-1, rows.shape[2]), mp, bank, bank_key)
        sums, counts = sums + new[:1], counts + about[0, 0]
        centroid = (count_old[:, None] * centroid_old + sums) / (count_old + counts)[:, None]
        back = lax.all_to_all(top, ALL, 0, 0, tiled=True)
        back = jnp.max(back.reshape(n_dp, n_mp, 2, -1), axis=1)[:, :, 0]
        best = jnp.maximum(best, jnp.max(jnp.where(here, back[:, :, None], -1.0), axis=(0, 1)))
        return about[0, 1], (best, sums, counts, centroid)

    blank = jnp.zeros((1, width), F32)
    most, state = one_round(ready, jnp.full((files,), -1.0, F32), blank, jnp.float32(0), blank)
    _, (best, _, _, centroid_new) = lax.while_loop(
        lambda s: 2 * s[0] < most.astype(I32),
        lambda s: (s[0] + 1, one_round(files_of(s[0]), *s[1])[1]),
        (jnp.int32(1), state),
    )
    return best, centroid_new


def solution(mesh):
    both = P(ALL)
    rows = P(ALL, None)
    return jax.shard_map(
        on_device,
        mesh=mesh,
        in_specs=(
            rows, P(), P(None, "mp"), P(None, "mp"), P("mp", None), both, both, both, P(), rows, both, both, rows, both,
        ),
        out_specs=(both, rows),
        check_vma=False,
    )
```

```python
import functools

import jax
import jax.numpy as jnp
from jax import lax
from jax.experimental import pallas as pl
from jax.experimental.pallas import tpu as pltpu
from jax.sharding import PartitionSpec as P

ALL = ("dp", "mp")
NX, NY, NZ, NC = 4, 4, 4, 2
ORDERS = 1 << 20
BF, F32, I32 = jnp.bfloat16, jnp.float32, jnp.int32
NT = (((1,), (1,)), ((), ()))


def from_x(v, j):
    perm = [(((x + j) % NX) * NY + y, x * NY + y) for x in range(NX) for y in range(NY)]
    return lax.ppermute(v, "mp", perm)


def from_y(v, k):
    perm = [(x * NY + (y + k) % NY, x * NY + y) for x in range(NX) for y in range(NY)]
    return lax.ppermute(v, "mp", perm)


def from_core(v):
    return lax.ppermute(v, "dp", [(d ^ 1, d) for d in range(NZ * NC)])


def block_ones(files, file_len, dtype):
    row = lax.broadcasted_iota(I32, (files, files * file_len), 0)
    col = lax.broadcasted_iota(I32, (files, files * file_len), 1)
    return jnp.where(col // file_len == row, 1.0, 0.0).astype(dtype)


def prep_kernel(file_len, len_ref, h_ref, gain_ref, n_ref, p_ref):
    gain = gain_ref[...].astype(F32)
    ones = jnp.ones((p_ref.shape[0], file_len), BF)
    for f in range(p_ref.shape[0]):
        rows = slice(f * file_len, (f + 1) * file_len)
        raw = h_ref[rows, :]
        resid = raw.astype(F32)
        scale = lax.rsqrt(jnp.mean(resid * resid, axis=-1, keepdims=True) + 1e-05)
        keep = lax.broadcasted_iota(I32, (file_len, 1), 0) < len_ref[f]
        n_ref[rows, :] = jnp.where(keep, resid * scale * gain, 0.0).astype(BF)
        valid = jnp.where(keep, resid, 0.0).astype(BF)
        p_ref[f:f + 1, :] = jnp.dot(ones, valid, preferred_element_type=F32)[:1]


def prep(hidden, gain, lengths):
    tok, width = hidden.shape
    files = lengths.shape[0]
    vm = pl.BlockSpec(memory_space=pltpu.VMEM)
    return pl.pallas_call(
        functools.partial(prep_kernel, tok // files),
        in_specs=[pl.BlockSpec(memory_space=pltpu.SMEM), vm, vm],
        out_specs=(vm, vm),
        out_shape=(jax.ShapeDtypeStruct((tok, width), BF), jax.ShapeDtypeStruct((files, width), F32)),
        compiler_params=pltpu.CompilerParams(vmem_limit_bytes=16 * 1024 * 1024),
        name="prep",
    )(lengths, hidden, gain[None, :])


def ffn_kernel(plan, n_tok, file_len, off_ref, *refs):
    n_parts = sum(len(p) for p, _ in plan)
    n_old = sum(1 for _, first in plan if first)
    toks, refs = refs[:n_tok], refs[n_tok:]
    parts, refs = refs[:n_parts], refs[n_parts:]
    olds, refs = list(refs[:n_old]), refs[n_old:]
    outs, refs = refs[:len(plan)], refs[len(plan):]
    t_buf, w_buf, t_sem, w_sem = refs
    hid = w_buf.shape[1] // 2

    def load_tokens():
        row, done = 0, []
        for t in range(n_tok):
            rows = toks[t].shape[0]
            done.append(pltpu.make_async_copy(toks[t], t_buf.at[pl.ds(row, rows)], t_sem.at[t]))
            done[-1].start()
            row += rows
        return done

    at, sem, waits = 0, 0, []
    for s, (pieces, _) in enumerate(plan):
        mine = []
        for p, n in enumerate(pieces):
            ref = parts[at + p]
            cols = ref.shape[-1]
            for q in range(n):
                start = pl.multiple_of(off_ref[sem], 128)
                src = ref.at[q] if len(ref.shape) == 3 else ref
                mine.append(pltpu.make_async_copy(src, w_buf.at[s, :, pl.ds(start, cols)], w_sem.at[sem]))
                mine[-1].start()
                sem += 1
        at += len(pieces)
        waits.append(mine)
        if s == 0:
            t_waits = load_tokens()
    for cp in t_waits:
        cp.wait()
    ones = block_ones(t_buf.shape[0] // file_len, file_len, BF)
    for s, (_, first) in enumerate(plan):
        for cp in waits[s]:
            cp.wait()
        both = lax.dot_general(w_buf[s], t_buf[...], NT, preferred_element_type=F32)
        gate = both[:hid]
        units = (0.5 * gate * (1.0 + jnp.tanh(0.5 * gate)) * both[hid:]).astype(BF)
        new = lax.dot_general(ones, units, NT, preferred_element_type=F32)
        if first:
            outs[s][:first // file_len, :] = olds.pop(0)[...]
        outs[s][first // file_len:, :] = new


def ffn(toks, slices, firsts, offs, file_len, name, olds=()):
    width = toks[0].shape[1]
    n_rows = sum(t.shape[0] for t in toks)
    rows = slices[0][0].shape[-2]
    plan = tuple((tuple(p.shape[0] if p.ndim == 3 else 1 for p in s), f) for s, f in zip(slices, firsts))
    flat = [p for s in slices for p in s]
    vm, hbm = pl.BlockSpec(memory_space=pltpu.VMEM), pl.BlockSpec(memory_space=pl.ANY)
    return pl.pallas_call(
        functools.partial(ffn_kernel, plan, len(toks), file_len),
        in_specs=[pl.BlockSpec(memory_space=pltpu.SMEM)] + [hbm] * (len(toks) + len(flat)) + [vm] * len(olds),
        out_specs=tuple(vm for _ in slices),
        out_shape=tuple(jax.ShapeDtypeStruct(((n_rows + f) // file_len, rows // 2), F32) for f in firsts),
        scratch_shapes=[
            pltpu.VMEM((n_rows, width), BF),
            pltpu.VMEM((len(slices), rows, width), BF),
            pltpu.SemaphoreType.DMA((len(toks),)),
            pltpu.SemaphoreType.DMA((sum(sum(p) for p, _ in plan),)),
        ],
        compiler_params=pltpu.CompilerParams(vmem_limit_bytes=(16 + 4 * len(slices)) * 1024 * 1024),
        name=name,
    )(offs, *toks, *flat, *olds)


def down_kernel(files, pos_ref, u0, u1, u2, u3, w_ref, o_ref, buf):
    for k, u in enumerate((u0, u1, u2, u3)):
        for j in range(NX):
            dst = pl.multiple_of(pos_ref[k * NX + j], files)
            buf[pl.ds(dst, files), :] = u[j * files:(j + 1) * files, :]
    rows = buf[...]
    hi = rows.astype(BF)
    lo = (rows - hi.astype(F32)).astype(BF)
    w = w_ref[...]
    term = jnp.dot(hi, w, preferred_element_type=F32) + jnp.dot(lo, w, preferred_element_type=F32)
    o_ref[...] = term.astype(BF).reshape(o_ref.shape)


def down(us, w_down, pos, files):
    rows = NX * NY * files
    vm = pl.BlockSpec(memory_space=pltpu.VMEM)
    return pl.pallas_call(
        functools.partial(down_kernel, files),
        in_specs=[pl.BlockSpec(memory_space=pltpu.SMEM)] + [vm] * 5,
        out_specs=vm,
        out_shape=jax.ShapeDtypeStruct((NX * NY, files, w_down.shape[1]), BF),
        scratch_shapes=[pltpu.VMEM((rows, us[0].shape[1]), F32)],
        compiler_params=pltpu.CompilerParams(vmem_limit_bytes=16 * 1024 * 1024),
        name="down",
    )(pos, *us, w_down)


def emb_kernel(copies, t_ref, p_ref, len_ref, sel_ref, meta_ref, o_ref):
    total = p_ref[...]
    for m in range(t_ref.shape[0]):
        total = total + t_ref[m].astype(F32)
    pooled = total / len_ref[...]
    norm = lax.rsqrt(jnp.sum(pooled * pooled, axis=-1, keepdims=True) + 1e-06)
    emb = (pooled * norm).astype(BF)
    width = emb.shape[1]
    rows = jnp.dot(sel_ref[...], emb, preferred_element_type=F32)
    for d in range(sel_ref.shape[0] // 2):
        pair = rows[2 * d:2 * d + 2, :].astype(BF)
        about = meta_ref[2 * d:2 * d + 2, :].astype(BF)
        for m in range(copies):
            o_ref[d * copies + m, :, :width] = pair
            o_ref[d * copies + m, :, width:] = about


def emb_to_owners(terms, pooled, lens, sel, meta, copies):
    return pl.pallas_call(
        functools.partial(emb_kernel, copies),
        out_shape=jax.ShapeDtypeStruct((sel.shape[0] // 2 * copies, 2, pooled.shape[1] + meta.shape[1]), BF),
        compiler_params=pltpu.CompilerParams(vmem_limit_bytes=16 * 1024 * 1024),
        name="emb",
    )(terms, pooled, lens, sel, meta)


def match_kernel(mp_ref, rows_ref, bank_ref, key_ref, best_ref, sums_ref, about_ref, buf, sem):
    width = bank_ref.shape[1]
    n_blocks = sem.shape[0]
    block = bank_ref.shape[0] // n_blocks
    copies = []
    for i in range(n_blocks):
        at = pl.ds(i * block, block)
        copies.append(pltpu.make_async_copy(bank_ref.at[at], buf.at[at], sem.at[i]))
        copies[-1].start()
    rows = rows_ref[:, :width]
    n = rows.shape[0]
    digits = rows_ref[:, width:].astype(F32)
    low = digits[:, 0:1] * 65536.0 + digits[:, 1:2] * 256.0 + digits[:, 2:3]
    high = digits[:, 3:4] * 65536.0 + digits[:, 4:5] * 256.0 + digits[:, 5:6]
    mine = jnp.where(digits[:, 6:7] == (mp_ref[0] + 1).astype(F32), 1.0, 0.0)
    member = jnp.broadcast_to(mine, (n, 8)).astype(BF)
    sums_ref[...] = lax.dot_general(member, rows, (((0,), (0,)), ((), ())), preferred_element_type=F32)
    count = jnp.sum(mine, axis=0, keepdims=True)
    most = jnp.max(digits[:, 7:8], axis=0, keepdims=True)
    about_ref[...] = jnp.where(lax.broadcasted_iota(I32, (1, 128), 1) == 0, count, most)
    best = jnp.full((n, 1), -1.0, F32)
    block *= n_blocks // 2
    for i in range(2):
        for cp in copies[i * n_blocks // 2:(i + 1) * n_blocks // 2]:
            cp.wait()
        at = slice(i * block, (i + 1) * block)
        sims = lax.dot_general(rows, buf[at, :], NT, preferred_element_type=F32)
        key = key_ref[:, at]
        best = jnp.maximum(best, jnp.max(jnp.where((key >= low) & (key < high), sims, -1.0), axis=1, keepdims=True))
    best_ref[:, 0, :] = jnp.broadcast_to(best, (n, 128))


def match(rows, mp, bank, key):
    vm = pl.BlockSpec(memory_space=pltpu.VMEM)
    return pl.pallas_call(
        match_kernel,
        in_specs=[pl.BlockSpec(memory_space=pltpu.SMEM), vm, pl.BlockSpec(memory_space=pl.ANY), vm],
        out_specs=(vm, vm, vm),
        out_shape=(
            jax.ShapeDtypeStruct((rows.shape[0], 1, 128), F32),
            jax.ShapeDtypeStruct((8, bank.shape[1]), F32),
            jax.ShapeDtypeStruct((1, 128), F32),
        ),
        scratch_shapes=[pltpu.VMEM(bank.shape, BF), pltpu.SemaphoreType.DMA((8,))],
        compiler_params=pltpu.CompilerParams(vmem_limit_bytes=24 * 1024 * 1024),
        name="match",
    )(mp[None], rows, bank, key)


def on_device(
    hidden_in,
    mlp_gain,
    w_gate,
    w_up,
    w_down,
    lengths,
    file_cluster,
    file_order,
    cluster_slot,
    bank,
    bank_slot,
    bank_order,
    centroid_old,
    count_old,
):
    tok, width = hidden_in.shape
    files = lengths.shape[0]
    file_len = tok // files
    n_dp, n_mp = NZ * NC, NX * NY
    dp, mp = lax.axis_index("dp"), lax.axis_index("mp")
    z, c, x, y = dp // NC, dp % NC, mp // NY, mp % NY
    tie = lax.optimization_barrier

    k_total = cluster_slot.shape[0]
    owned = k_total // n_dp
    lookup = file_cluster[:, None] == jnp.arange(k_total, dtype=I32)[None, :]
    slot = jnp.sum(jnp.where(lookup, cluster_slot[None, :], 0), axis=1)
    owner = slot // owned
    ids = jnp.arange(files, dtype=I32)
    rank = jnp.sum(((owner[:, None] == owner[None, :]) & (ids[None, :] < ids[:, None])).astype(I32), axis=1)
    place = (owner[None, None, :] == jnp.arange(n_dp, dtype=I32)[:, None, None]) & (
        rank[None, None, :] == ids[None, :, None]
    )
    local = slot % owned
    first = local * ORDERS
    key = first + file_order
    bank_key = (bank_slot * ORDERS + bank_order).astype(F32)[None, :]
    low_key, high_key = [first >> 16, first * 0, first * 0], [key >> 16, (key >> 8) & 255, key & 255]
    digits = jnp.stack(low_key + high_key + [local + 1, jnp.broadcast_to(jnp.max(rank) + 1, slot.shape)], axis=1)

    def files_of(r):
        here = lax.dynamic_slice_in_dim(place, 2 * r, 2, 1)
        sel = here.reshape(-1, files)
        meta = jnp.sum(jnp.where(sel[:, :, None], digits[None], 0), axis=1).astype(F32)
        return here, sel.astype(BF), jnp.pad(meta, ((0, 0), (0, 120)))

    half, quarter = width // 2, width // 4
    w_t = [w_gate.T, w_up.T]
    w_h = jnp.concatenate([lax.dynamic_slice_in_dim(w, c * half, half, 1) for w in w_t], axis=0)
    w_h, hidden_in, w_t = tie((w_h, hidden_in, w_t))
    normed, pooled_in = prep(hidden_in, mlp_gain, lengths)
    t1, t3 = from_x(normed, 1), from_x(normed, 3)
    h1, h3 = from_y(w_h, 1), from_y(w_h, 3)
    w_own = jnp.concatenate(w_t, axis=0)
    t1, t3 = tie((t1, t3))
    t2a, t2b = from_x(t1[:tok // 2], 1), from_x(t3[tok // 2:], 3)
    toks, last = [normed, t1, t3], [t2a, t2b]

    h_off = jnp.stack([c * half, (1 - c) * half]).astype(I32)
    e_off = jnp.stack([k * half + q * quarter for k in (c, 1 - c) for q in (0, 1)]).astype(I32)
    pos = jnp.stack(
        [(((x + j) % NX) * NY + (y - k) % NY) * files for k in range(NY) for j in (0, 1, 3, 2)]
    ).astype(I32)
    lens = lengths.astype(F32)[:, None]
    ready = files_of(0)
    normed, e_off, h_off, pos, lens, bank_key, ready = tie((normed, e_off, h_off, pos, lens, bank_key, ready))
    toks[0] = normed

    zero = jnp.zeros((1,), I32)
    (u0,) = ffn(toks, [[w_own]], (0,), zero, file_len, "ffn_own")
    h1, h3, u0 = tie((h1, h3, u0))
    k2a, k2b = from_y(h1[:, :quarter], 1), from_y(h3[:, quarter:], 3)
    near = [[h1, from_core(h1)], [h3, from_core(h3)]]
    near_off = jnp.concatenate([h_off, h_off])
    u1, u3 = ffn(toks, near, (0, 0), near_off, file_len, "ffn_near")
    first = sum(t.shape[0] for t in toks)
    k2a, k2b, u1, u3, last = tie((k2a, k2b, u1, u3, last))
    far = [k2a, k2b, from_core(k2a), from_core(k2b)]
    rest = jnp.concatenate([near_off, zero])
    u1, u3, u0 = ffn(last, near + [[w_own]], (first,) * 3, rest, file_len, "ffn_rest", (u1, u3, u0))
    r1, r3 = from_y(u1, NY - 1), from_y(u3, NY - 3)
    (u2,) = ffn(toks + last, [far], (0,), e_off, file_len, "ffn_far")
    r2 = from_y(u2, NY - 2)
    terms = down([u0, r1, r2, r3], w_down, pos, files)
    terms = lax.all_to_all(terms, "mp", 0, 0, tiled=True)

    def one_round(ready, best, sums, counts, _):
        here, sel, meta = ready
        rows = emb_to_owners(terms, pooled_in, lens, sel, meta, n_mp)
        rows = lax.all_to_all(rows, ALL, 0, 0, tiled=True)
        top, new, about = match(rows.reshape(-1, rows.shape[2]), mp, bank, bank_key)
        sums, counts = sums + new[:1], counts + about[0, 0]
        centroid = (count_old[:, None] * centroid_old + sums) / (count_old + counts)[:, None]
        back = lax.all_to_all(top, ALL, 0, 0, tiled=True)
        back = jnp.max(back.reshape(n_dp, n_mp, 2, -1), axis=1)[:, :, 0]
        best = jnp.maximum(best, jnp.max(jnp.where(here, back[:, :, None], -1.0), axis=(0, 1)))
        return about[0, 1], (best, sums, counts, centroid)

    blank = jnp.zeros((1, width), F32)
    most, state = one_round(ready, jnp.full((files,), -1.0, F32), blank, jnp.float32(0), blank)
    _, (best, _, _, centroid_new) = lax.while_loop(
        lambda s: 2 * s[0] < most.astype(I32),
        lambda s: (s[0] + 1, one_round(files_of(s[0]), *s[1])[1]),
        (jnp.int32(1), state),
    )
    return best, centroid_new


def solution(mesh):
    both = P(ALL)
    rows = P(ALL, None)
    return jax.shard_map(
        on_device,
        mesh=mesh,
        in_specs=(
            rows, P(), P(None, "mp"), P(None, "mp"), P("mp", None), both, both, both, P(), rows, both, both, rows, both,
        ),
        out_specs=(both, rows),
        check_vma=False,
    )
```

```python
import functools

import jax
import jax.numpy as jnp
from jax import lax
from jax.experimental import pallas as pl
from jax.experimental.pallas import tpu as pltpu
from jax.sharding import PartitionSpec as P

ALL = ("dp", "mp")
NX, NY, NZ, NC = 4, 4, 4, 2
ORDERS = 1 << 20
BF, F32, I32 = jnp.bfloat16, jnp.float32, jnp.int32
NT = (((1,), (1,)), ((), ()))


def from_x(v, j):
    perm = [(((x + j) % NX) * NY + y, x * NY + y) for x in range(NX) for y in range(NY)]
    return lax.ppermute(v, "mp", perm)


def from_y(v, k):
    perm = [(x * NY + (y + k) % NY, x * NY + y) for x in range(NX) for y in range(NY)]
    return lax.ppermute(v, "mp", perm)


def from_core(v):
    return lax.ppermute(v, "dp", [(d ^ 1, d) for d in range(NZ * NC)])


def block_ones(files, file_len, dtype):
    row = lax.broadcasted_iota(I32, (files, files * file_len), 0)
    col = lax.broadcasted_iota(I32, (files, files * file_len), 1)
    return jnp.where(col // file_len == row, 1.0, 0.0).astype(dtype)


def prep_kernel(file_len, len_ref, h_ref, gain_ref, n_ref, p_ref):
    gain = gain_ref[...].astype(F32)
    ones = jnp.ones((p_ref.shape[0], file_len), BF)
    for f in range(p_ref.shape[0]):
        rows = slice(f * file_len, (f + 1) * file_len)
        raw = h_ref[rows, :]
        resid = raw.astype(F32)
        scale = lax.rsqrt(jnp.mean(resid * resid, axis=-1, keepdims=True) + 1e-05)
        keep = lax.broadcasted_iota(I32, (file_len, 1), 0) < len_ref[f]
        n_ref[rows, :] = jnp.where(keep, resid * scale * gain, 0.0).astype(BF)
        valid = jnp.where(keep, resid, 0.0).astype(BF)
        p_ref[f:f + 1, :] = jnp.dot(ones, valid, preferred_element_type=F32)[:1]


def prep(hidden, gain, lengths):
    tok, width = hidden.shape
    files = lengths.shape[0]
    vm = pl.BlockSpec(memory_space=pltpu.VMEM)
    return pl.pallas_call(
        functools.partial(prep_kernel, tok // files),
        in_specs=[pl.BlockSpec(memory_space=pltpu.SMEM), vm, vm],
        out_specs=(vm, vm),
        out_shape=(jax.ShapeDtypeStruct((tok, width), BF), jax.ShapeDtypeStruct((files, width), F32)),
        compiler_params=pltpu.CompilerParams(vmem_limit_bytes=16 * 1024 * 1024),
        name="prep",
    )(lengths, hidden, gain[None, :])


def ffn_kernel(plan, n_tok, file_len, off_ref, *refs):
    n_parts = sum(len(p) for p, _ in plan)
    n_old = sum(1 for _, first in plan if first)
    toks, refs = refs[:n_tok], refs[n_tok:]
    parts, refs = refs[:n_parts], refs[n_parts:]
    olds, refs = list(refs[:n_old]), refs[n_old:]
    outs, refs = refs[:len(plan)], refs[len(plan):]
    t_buf, w_buf, t_sem, w_sem = refs
    hid = w_buf.shape[1] // 2

    def load_tokens():
        row, done = 0, []
        for t in range(n_tok):
            rows = toks[t].shape[0]
            done.append(pltpu.make_async_copy(toks[t], t_buf.at[pl.ds(row, rows)], t_sem.at[t]))
            done[-1].start()
            row += rows
        return done

    at, sem, waits = 0, 0, []
    for s, (pieces, _) in enumerate(plan):
        mine = []
        for p, n in enumerate(pieces):
            ref = parts[at + p]
            cols = ref.shape[-1]
            for q in range(n):
                start = pl.multiple_of(off_ref[sem], 128)
                src = ref.at[q] if len(ref.shape) == 3 else ref
                mine.append(pltpu.make_async_copy(src, w_buf.at[s, :, pl.ds(start, cols)], w_sem.at[sem]))
                mine[-1].start()
                sem += 1
        at += len(pieces)
        waits.append(mine)
        if s == 0:
            t_waits = load_tokens()
    for cp in t_waits:
        cp.wait()
    ones = block_ones(t_buf.shape[0] // file_len, file_len, BF)
    for s, (_, first) in enumerate(plan):
        for cp in waits[s]:
            cp.wait()
        both = lax.dot_general(w_buf[s], t_buf[...], NT, preferred_element_type=F32)
        gate = both[:hid]
        units = (0.5 * gate * (1.0 + jnp.tanh(0.5 * gate)) * both[hid:]).astype(BF)
        new = lax.dot_general(ones, units, NT, preferred_element_type=F32)
        if first:
            outs[s][:first // file_len, :] = olds.pop(0)[...]
        outs[s][first // file_len:, :] = new


def ffn(toks, slices, firsts, offs, file_len, name, olds=()):
    width = toks[0].shape[1]
    n_rows = sum(t.shape[0] for t in toks)
    rows = slices[0][0].shape[-2]
    plan = tuple((tuple(p.shape[0] if p.ndim == 3 else 1 for p in s), f) for s, f in zip(slices, firsts))
    flat = [p for s in slices for p in s]
    vm, hbm = pl.BlockSpec(memory_space=pltpu.VMEM), pl.BlockSpec(memory_space=pl.ANY)
    return pl.pallas_call(
        functools.partial(ffn_kernel, plan, len(toks), file_len),
        in_specs=[pl.BlockSpec(memory_space=pltpu.SMEM)] + [hbm] * (len(toks) + len(flat)) + [vm] * len(olds),
        out_specs=tuple(vm for _ in slices),
        out_shape=tuple(jax.ShapeDtypeStruct(((n_rows + f) // file_len, rows // 2), F32) for f in firsts),
        scratch_shapes=[
            pltpu.VMEM((n_rows, width), BF),
            pltpu.VMEM((len(slices), rows, width), BF),
            pltpu.SemaphoreType.DMA((len(toks),)),
            pltpu.SemaphoreType.DMA((sum(sum(p) for p, _ in plan),)),
        ],
        compiler_params=pltpu.CompilerParams(vmem_limit_bytes=(16 + 4 * len(slices)) * 1024 * 1024),
        name=name,
    )(offs, *toks, *flat, *olds)


def down_kernel(files, pos_ref, u0, u1, u2, u3, w_ref, o_ref, buf):
    for k, u in enumerate((u0, u1, u2, u3)):
        for j in range(NX):
            dst = pl.multiple_of(pos_ref[k * NX + j], files)
            buf[pl.ds(dst, files), :] = u[j * files:(j + 1) * files, :]
    rows = buf[...]
    hi = rows.astype(BF)
    lo = (rows - hi.astype(F32)).astype(BF)
    w = w_ref[...]
    term = jnp.dot(hi, w, preferred_element_type=F32) + jnp.dot(lo, w, preferred_element_type=F32)
    o_ref[...] = term.astype(BF).reshape(o_ref.shape)


def down(us, w_down, pos, files):
    rows = NX * NY * files
    vm = pl.BlockSpec(memory_space=pltpu.VMEM)
    return pl.pallas_call(
        functools.partial(down_kernel, files),
        in_specs=[pl.BlockSpec(memory_space=pltpu.SMEM)] + [vm] * 5,
        out_specs=vm,
        out_shape=jax.ShapeDtypeStruct((NX * NY, files, w_down.shape[1]), BF),
        scratch_shapes=[pltpu.VMEM((rows, us[0].shape[1]), F32)],
        compiler_params=pltpu.CompilerParams(vmem_limit_bytes=16 * 1024 * 1024),
        name="down",
    )(pos, *us, w_down)


def emb_kernel(copies, t_ref, p_ref, len_ref, sel_ref, meta_ref, o_ref):
    total = p_ref[...]
    for m in range(t_ref.shape[0]):
        total = total + t_ref[m].astype(F32)
    pooled = total / len_ref[...]
    norm = lax.rsqrt(jnp.sum(pooled * pooled, axis=-1, keepdims=True) + 1e-06)
    emb = (pooled * norm).astype(BF)
    width = emb.shape[1]
    rows = jnp.dot(sel_ref[...], emb, preferred_element_type=F32)
    for d in range(sel_ref.shape[0] // 2):
        pair = rows[2 * d:2 * d + 2, :].astype(BF)
        about = meta_ref[2 * d:2 * d + 2, :].astype(BF)
        for m in range(copies):
            o_ref[d * copies + m, :, :width] = pair
            o_ref[d * copies + m, :, width:] = about


def emb_to_owners(terms, pooled, lens, sel, meta, copies):
    return pl.pallas_call(
        functools.partial(emb_kernel, copies),
        out_shape=jax.ShapeDtypeStruct((sel.shape[0] // 2 * copies, 2, pooled.shape[1] + meta.shape[1]), BF),
        compiler_params=pltpu.CompilerParams(vmem_limit_bytes=16 * 1024 * 1024),
        name="emb",
    )(terms, pooled, lens, sel, meta)


def match_kernel(mp_ref, rows_ref, bank_ref, key_ref, best_ref, sums_ref, about_ref, buf, sem):
    width = bank_ref.shape[1]
    n_blocks = sem.shape[0]
    block = bank_ref.shape[0] // n_blocks
    copies = []
    for i in range(n_blocks):
        at = pl.ds(i * block, block)
        copies.append(pltpu.make_async_copy(bank_ref.at[at], buf.at[at], sem.at[i]))
        copies[-1].start()
    rows = rows_ref[:, :width]
    n = rows.shape[0]
    digits = rows_ref[:, width:].astype(F32)
    low = digits[:, 0:1] * 65536.0 + digits[:, 1:2] * 256.0 + digits[:, 2:3]
    high = digits[:, 3:4] * 65536.0 + digits[:, 4:5] * 256.0 + digits[:, 5:6]
    mine = jnp.where(digits[:, 6:7] == (mp_ref[0] + 1).astype(F32), 1.0, 0.0)
    member = jnp.broadcast_to(mine, (n, 8)).astype(BF)
    sums_ref[...] = lax.dot_general(member, rows, (((0,), (0,)), ((), ())), preferred_element_type=F32)
    count = jnp.sum(mine, axis=0, keepdims=True)
    most = jnp.max(digits[:, 7:8], axis=0, keepdims=True)
    about_ref[...] = jnp.where(lax.broadcasted_iota(I32, (1, 128), 1) == 0, count, most)
    best = jnp.full((n, 1), -1.0, F32)
    block *= n_blocks // 2
    for i in range(2):
        for cp in copies[i * n_blocks // 2:(i + 1) * n_blocks // 2]:
            cp.wait()
        at = slice(i * block, (i + 1) * block)
        sims = lax.dot_general(rows, buf[at, :], NT, preferred_element_type=F32)
        key = key_ref[:, at]
        best = jnp.maximum(best, jnp.max(jnp.where((key >= low) & (key < high), sims, -1.0), axis=1, keepdims=True))
    best_ref[:, 0, :] = jnp.broadcast_to(best, (n, 128))


def match(rows, mp, bank, key):
    vm = pl.BlockSpec(memory_space=pltpu.VMEM)
    return pl.pallas_call(
        match_kernel,
        in_specs=[pl.BlockSpec(memory_space=pltpu.SMEM), vm, pl.BlockSpec(memory_space=pl.ANY), vm],
        out_specs=(vm, vm, vm),
        out_shape=(
            jax.ShapeDtypeStruct((rows.shape[0], 1, 128), F32),
            jax.ShapeDtypeStruct((8, bank.shape[1]), F32),
            jax.ShapeDtypeStruct((1, 128), F32),
        ),
        scratch_shapes=[pltpu.VMEM(bank.shape, BF), pltpu.SemaphoreType.DMA((8,))],
        compiler_params=pltpu.CompilerParams(vmem_limit_bytes=24 * 1024 * 1024),
        name="match",
    )(mp[None], rows, bank, key)


def on_device(
    hidden_in,
    mlp_gain,
    w_gate,
    w_up,
    w_down,
    lengths,
    file_cluster,
    file_order,
    cluster_slot,
    bank,
    bank_slot,
    bank_order,
    centroid_old,
    count_old,
):
    tok, width = hidden_in.shape
    files = lengths.shape[0]
    file_len = tok // files
    n_dp, n_mp = NZ * NC, NX * NY
    dp, mp = lax.axis_index("dp"), lax.axis_index("mp")
    z, c, x, y = dp // NC, dp % NC, mp // NY, mp % NY
    tie = lax.optimization_barrier

    k_total = cluster_slot.shape[0]
    owned = k_total // n_dp
    lookup = file_cluster[:, None] == jnp.arange(k_total, dtype=I32)[None, :]
    slot = jnp.sum(jnp.where(lookup, cluster_slot[None, :], 0), axis=1)
    owner = slot // owned
    ids = jnp.arange(files, dtype=I32)
    rank = jnp.sum(((owner[:, None] == owner[None, :]) & (ids[None, :] < ids[:, None])).astype(I32), axis=1)
    place = (owner[None, None, :] == jnp.arange(n_dp, dtype=I32)[:, None, None]) & (
        rank[None, None, :] == ids[None, :, None]
    )
    local = slot % owned
    first = local * ORDERS
    key = first + file_order
    bank_key = (bank_slot * ORDERS + bank_order).astype(F32)[None, :]
    low_key, high_key = [first >> 16, first * 0, first * 0], [key >> 16, (key >> 8) & 255, key & 255]
    digits = jnp.stack(low_key + high_key + [local + 1, jnp.broadcast_to(jnp.max(rank) + 1, slot.shape)], axis=1)

    def files_of(r):
        here = lax.dynamic_slice_in_dim(place, 2 * r, 2, 1)
        sel = here.reshape(-1, files)
        meta = jnp.sum(jnp.where(sel[:, :, None], digits[None], 0), axis=1).astype(F32)
        return here, sel.astype(BF), jnp.pad(meta, ((0, 0), (0, 120)))

    half, quarter = width // 2, width // 4
    w_t = [w_gate.T, w_up.T]
    w_h = jnp.concatenate([lax.dynamic_slice_in_dim(w, c * half, half, 1) for w in w_t], axis=0)
    w_h, hidden_in, w_t = tie((w_h, hidden_in, w_t))
    normed, pooled_in = prep(hidden_in, mlp_gain, lengths)
    t1, t3 = from_x(normed, 1), from_x(normed, 3)
    h1, h3 = from_y(w_h, 1), from_y(w_h, 3)
    w_own = jnp.concatenate(w_t, axis=0)
    t1, t3 = tie((t1, t3))
    t2a, t2b = from_x(t1[:tok // 2], 1), from_x(t3[tok // 2:], 3)
    toks, last = [normed, t1, t3], [t2a, t2b]

    h_off = jnp.stack([c * half, (1 - c) * half]).astype(I32)
    e_off = jnp.stack([k * half + q * quarter for k in (c, 1 - c) for q in (0, 1)]).astype(I32)
    pos = jnp.stack(
        [(((x + j) % NX) * NY + (y - k) % NY) * files for k in range(NY) for j in (0, 1, 3, 2)]
    ).astype(I32)
    lens = lengths.astype(F32)[:, None]
    ready = files_of(0)
    normed, e_off, h_off, pos, lens, bank_key, ready = tie((normed, e_off, h_off, pos, lens, bank_key, ready))
    toks[0] = normed

    zero = jnp.zeros((1,), I32)
    (u0,) = ffn(toks, [[w_own]], (0,), zero, file_len, "ffn_own")
    h1, h3, u0 = tie((h1, h3, u0))
    k2a, k2b = from_y(h1[:, :quarter], 1), from_y(h3[:, quarter:], 3)
    near = [[h1, from_core(h1)], [h3, from_core(h3)]]
    near_off = jnp.concatenate([h_off, h_off])
    u1, u3 = ffn(toks, near, (0, 0), near_off, file_len, "ffn_near")
    first = sum(t.shape[0] for t in toks)
    k2a, k2b, u1, u3, last = tie((k2a, k2b, u1, u3, last))
    far = [k2a, k2b, from_core(k2a), from_core(k2b)]
    rest = jnp.concatenate([near_off, zero])
    u1, u3, u0 = ffn(last, near + [[w_own]], (first,) * 3, rest, file_len, "ffn_rest", (u1, u3, u0))
    r1, r3 = from_y(u1, NY - 1), from_y(u3, NY - 3)
    (u2,) = ffn(toks + last, [far], (0,), e_off, file_len, "ffn_far")
    r2 = from_y(u2, NY - 2)
    terms = down([u0, r1, r2, r3], w_down, pos, files)
    terms = lax.all_to_all(terms, "mp", 0, 0, tiled=True)

    def one_round(ready, best, sums, counts):
        here, sel, meta = ready
        rows = emb_to_owners(terms, pooled_in, lens, sel, meta, n_mp)
        rows = lax.all_to_all(rows, ALL, 0, 0, tiled=True)
        top, new, about = match(rows.reshape(-1, rows.shape[2]), mp, bank, bank_key)
        back = lax.all_to_all(top, ALL, 0, 0, tiled=True)
        back = jnp.max(back.reshape(n_dp, n_mp, 2, -1), axis=1)[:, :, 0]
        best = jnp.maximum(best, jnp.max(jnp.where(here, back[:, :, None], -1.0), axis=(0, 1)))
        return about[0, 1], (best, sums + new[:1], counts + about[0, 0])

    most, state = one_round(ready, jnp.full((files,), -1.0, F32), jnp.zeros((1, width), F32), jnp.float32(0))
    _, (best, sums, counts) = lax.while_loop(
        lambda s: 2 * s[0] < most.astype(I32),
        lambda s: (s[0] + 1, one_round(files_of(s[0]), *s[1])[1]),
        (jnp.int32(1), state),
    )
    centroid_new = (count_old[:, None] * centroid_old + sums) / (count_old + counts)[:, None]
    return best, centroid_new


def solution(mesh):
    both = P(ALL)
    rows = P(ALL, None)
    return jax.shard_map(
        on_device,
        mesh=mesh,
        in_specs=(
            rows, P(), P(None, "mp"), P(None, "mp"), P("mp", None), both, both, both, P(), rows, both, both, rows, both,
        ),
        out_specs=(both, rows),
        check_vma=False,
    )
```
